32 devices in a mesh: dom: 8 (over z, x), group: 4 (over y, core).
Axes of the slice: x: 2, y: 2, z: 4, core: 2. Of those that a mesh axis runs over, the one named last changes fastest.
Arguments:
- embeddings: float32 [131072, 256], P(('dom', 'group')), may hold values from -0.5 to 0.5
- adagrad_state: float32 [131072], P(('dom', 'group')), may hold values from 0.001 to 0.1
- edge_count: int32 [8], P('dom'), may hold values from 1 to 4096
- lhs_owner: int32 [8, 4, 1024, 1], P('dom', 'group'), may hold values from 0 to 31; in each aligned block of 1024 rows (0 to 1023, 1024 to 2047, ..., all dimensions but the last counted through in order) at most 40 rows name the same one
- lhs_row: int32 [8, 4, 1024], P('dom', 'group'), may hold values from 0 to 4095
- rhs_owner: int32 [8, 4, 1024, 1], P('dom', 'group'), may hold values from 0 to 31; in each aligned block of 1024 rows (0 to 1023, 1024 to 2047, ..., all dimensions but the last counted through in order) at most 40 rows name the same one
- rhs_row: int32 [8, 4, 1024], P('dom', 'group'), may hold values from 0 to 4095
- neg_owner: int32 [8, 4, 1024, 1], P('dom', 'group'), may hold values from 0 to 31; in each aligned block of 1024 rows (0 to 1023, 1024 to 2047, ..., all dimensions but the last counted through in order) at most 40 rows name the same one
- neg_row: int32 [8, 4, 1024], P('dom', 'group'), may hold values from 0 to 4095
Outputs:
- new_embeddings: float32 [131072, 256], P(('dom', 'group'))
- new_state: float32 [131072], P(('dom', 'group'))
The draws below stay inside these ranges and needn't reach their ends.
Inputs may be any that keep to these rules, and one draw needn't show every extreme that they name: `lhs_owner`: in each group (aligned block of 1024 entries) no device number is named more than 40 times. `rhs_owner`: in each group (aligned block of 1024 entries) no device number is named more than 40 times. `neg_owner`: in each group (aligned block of 1024 entries) no device number is named more than 40 times.
All inputs are finite; a program needn't handle non-finite values.
Results may differ from the reference program's by a relative error of at most 0.00077.
Values may be sent and summed in bfloat16 or wider, within the bound.
No kernel may reach another device: no remote copies, remote signals or barrier semaphores. Data moves between devices by JAX's collectives and lax.ppermute only.
A program may use at most 64 MiB of HBM per device.

```python
import math
import jax
import jax.numpy as jnp
import numpy as np
from jax import lax

D = 256
CE = 1024
NEG = 1024
ROWS_DEV = 4096
SLOTS = 4
MOST = 40
ENTITIES = 131072
N_DOM = 8
DEVICES = 32


def with_ends(values, stream_key, low, largest):
    dims = values.shape
    spot = [jax.random.randint(jax.random.fold_in(stream_key, axis), (), 0, dims[axis]) for axis in range(len(dims))]
    values = values.at[tuple(spot)].set(low)
    longest = dims.index(max(dims))
    spot[longest] = (spot[longest] + 1) % dims[longest]
    return values.at[tuple(spot)].set(largest)


def shard_levels(key, shape, cuts, smallest, largest):
    gain, own = 1.0, jax.random.fold_in(key, 6)
    for dim, blocks in cuts:
        steps = jnp.exp(jax.random.uniform(jax.random.fold_in(own, dim), (blocks,), jnp.float32, smallest / len(cuts), largest / len(cuts)))
        gain = gain * jnp.repeat(steps, shape[dim] // blocks).reshape([-1 if axis == dim else 1 for axis in range(len(shape))])
    return gain


def assign_block(key, own, number, rows, amount, top, limit, lean):
    order = jax.random.permutation(key, amount)
    packed, ordinary = portions_of(amount, rows * top, limit, lean, True), portions_of(amount, rows * top, limit, lean, False)
    places = jnp.arange(amount)

    def named(tallies, rotation):
        used = int((tallies > 0).sum())
        fixed = max(1, used // 4)
        moved = fixed + (places - fixed + rotation * (used - fixed)) % max(1, amount - fixed)
        return jnp.zeros((amount,), jnp.int32).at[order[jnp.where(places < fixed, places, moved)]].set(jnp.asarray(tallies, jnp.int32))

    tallies = jnp.where(number % 4 == 0, named(packed, number // 4), named(ordinary, number - number // 4 - 1))
    mixed = jax.random.permutation(jax.random.fold_in(own, 3), amount)
    source_of, taker = mixed[0:amount // 2 * 2:2], mixed[1:amount // 2 * 2:2]
    room = jnp.minimum(tallies[source_of] - 1, limit - tallies[taker]) // 2
    room = jnp.where((source_of == order[0]) | (taker == order[0]) | (tallies[taker] == 0), 0, jnp.maximum(room, 0))
    moved = jax.random.randint(jax.random.fold_in(own, 4), (amount // 2,), 0, 1 << 20) % (room + 1)
    tallies = tallies.at[source_of].add(-moved).at[taker].add(moved)
    members = jnp.searchsorted(jnp.cumsum(tallies), jnp.arange(rows * top), side="right").astype(jnp.int32)
    grid = members.reshape(top, rows).T
    grid = grid[jax.random.permutation(jax.random.fold_in(own, 1), rows)]
    rotation = jax.random.randint(jax.random.fold_in(own, 2), (rows, 1), 0, top)
    return jnp.take_along_axis(grid, (jnp.arange(top)[None, :] + rotation) % top, axis=1)


def portions_of(number_of, total, most, skew, full):
    weights = [(1 << 20) // math.isqrt(grade ** skew) + 1 for grade in range(1, number_of + 1)]
    largest = most if full else min(most, max(-(-total // number_of), total * weights[0] // sum(weights)))
    least = 1 if total - largest >= number_of - 1 else 0
    given, surplus = [largest] + [least] * (number_of - 1), total - largest - least * (number_of - 1)
    while surplus > 0:
        movable = [i for i in range(1, number_of) if given[i] < largest] or [i for i in range(1, number_of) if given[i] < most]
        whole, left = sum([weights[i] for i in movable]), surplus
        for i in movable:
            extra = min(most - given[i], max(1, left * weights[i] // whole), surplus)
            given[i] = given[i] + extra
            surplus = surplus - extra
    return np.array(given)


def gaussian(stream_key, shape, deviation, reach, cuts=(), held_as=jnp.bfloat16):
    result = jax.random.normal(stream_key, shape, jnp.float32) * deviation
    if len(cuts) > 0:
        result = shard_levels(stream_key, shape, cuts, -0.22, 0.18) * result
    return jnp.clip(result, min=-reach, max=reach).astype(held_as)


def setup_inputs(seed: int = 0) -> dict:
    key_of = jax.random.split(jax.random.key(seed), 10)
    embeddings = gaussian(key_of[0], (ENTITIES, D), 0.2, 0.5, ((0, 32),), jnp.float32)
    adagrad_state = jnp.clip(jnp.exp(math.log(0.1) - 4.6051702 * jax.random.uniform(key_of[1], (ENTITIES,), jnp.float32) ** shard_levels(key_of[1], (ENTITIES,), ((0, 32),), -0.2, 0.2)), 0.001, 0.1)
    edge_count = with_ends(jax.random.randint(key_of[2], (N_DOM,), 1, SLOTS * CE + 1), jax.random.fold_in(key_of[2], 1), 1, SLOTS * CE).astype(jnp.int32)
    lhs_owner_keys = jax.random.split(jax.random.fold_in(key_of[3], 1), N_DOM * SLOTS * CE // CE)
    lhs_owner_turns = jax.random.permutation(jax.random.fold_in(key_of[3], 3), N_DOM * SLOTS * CE // CE)
    lhs_owner = jax.vmap(lambda own, number: assign_block(jax.random.fold_in(key_of[3], 2), own, number, CE, DEVICES, 1, MOST, 1))(lhs_owner_keys, lhs_owner_turns).reshape((N_DOM, SLOTS, CE, 1))
    lhs_row = with_ends(jax.random.randint(key_of[4], (N_DOM, SLOTS, CE), 0, ROWS_DEV), jax.random.fold_in(key_of[4], 1), 0, ROWS_DEV - 1).astype(jnp.int32)
    rhs_owner_keys = jax.random.split(jax.random.fold_in(key_of[5], 1), N_DOM * SLOTS * CE // CE)
    rhs_owner_turns = jax.random.permutation(jax.random.fold_in(key_of[5], 3), N_DOM * SLOTS * CE // CE)
    rhs_owner = jax.vmap(lambda own, number: assign_block(jax.random.fold_in(key_of[5], 2), own, number, CE, DEVICES, 1, MOST, 1))(rhs_owner_keys, rhs_owner_turns).reshape((N_DOM, SLOTS, CE, 1))
    rhs_row = with_ends(jax.random.randint(key_of[6], (N_DOM, SLOTS, CE), 0, ROWS_DEV), jax.random.fold_in(key_of[6], 1), 0, ROWS_DEV - 1).astype(jnp.int32)
    neg_owner_keys = jax.random.split(jax.random.fold_in(key_of[7], 1), N_DOM * SLOTS * NEG // NEG)
    neg_owner_turns = jax.random.permutation(jax.random.fold_in(key_of[7], 3), N_DOM * SLOTS * NEG // NEG)
    neg_owner = jax.vmap(lambda own, number: assign_block(jax.random.fold_in(key_of[7], 2), own, number, NEG, DEVICES, 1, MOST, 1))(neg_owner_keys, neg_owner_turns).reshape((N_DOM, SLOTS, NEG, 1))
    neg_row = with_ends(jax.random.randint(key_of[8], (N_DOM, SLOTS, NEG), 0, ROWS_DEV), jax.random.fold_in(key_of[8], 1), 0, ROWS_DEV - 1).astype(jnp.int32)
    return dict(embeddings=embeddings, adagrad_state=adagrad_state, edge_count=edge_count, lhs_owner=lhs_owner, lhs_row=lhs_row, rhs_owner=rhs_owner, rhs_row=rhs_row, neg_owner=neg_owner, neg_row=neg_row)


learn_rate = 0.1
adagrad_eps = 1e-06

def group_gradients(left_rows, right_rows, shared_rows, live_limit):
    left_wide = left_rows.astype(jnp.float32)
    right_wide = right_rows.astype(jnp.float32)
    positive = lax.optimization_barrier(jnp.sum(left_wide * right_wide, axis=1))
    contract = (((1,), (1,)), ((), ()))
    across = (((0,), (0,)), ((), ()))
    shared = lax.dot_general(left_rows, shared_rows, contract, preferred_element_type=jnp.float32)
    inchunk = lax.dot_general(left_rows, right_rows, contract, preferred_element_type=jnp.float32)
    places = jnp.arange(left_rows.shape[0], dtype=jnp.int32)
    live_mask = (places < live_limit).astype(jnp.float32)
    allowed = live_mask[None, :] * (places[:, None] != places[None, :]).astype(jnp.float32)
    pos_exp = jnp.exp(positive)
    shared_exp = jnp.exp(shared)
    inchunk_exp = jnp.exp(inchunk) * allowed
    totals = pos_exp + lax.optimization_barrier(jnp.sum(shared_exp, axis=1)) + lax.optimization_barrier(jnp.sum(inchunk_exp, axis=1))
    weights = live_mask / totals
    pos_grad = live_mask * (pos_exp / totals - 1.0)
    shared_prob = (shared_exp * weights[:, None]).astype(jnp.bfloat16)
    inchunk_prob = (inchunk_exp * weights[:, None]).astype(jnp.bfloat16)
    grad_left = pos_grad[:, None] * right_wide + jnp.dot(shared_prob, shared_rows, preferred_element_type=jnp.float32) + jnp.dot(inchunk_prob, right_rows, preferred_element_type=jnp.float32)
    grad_right = pos_grad[:, None] * left_wide + lax.dot_general(inchunk_prob, left_rows, across, preferred_element_type=jnp.float32)
    grad_shared = lax.dot_general(shared_prob, left_rows, across, preferred_element_type=jnp.float32)
    return (grad_left.astype(jnp.bfloat16), grad_right.astype(jnp.bfloat16), grad_shared.astype(jnp.bfloat16))

def reference(embeddings, adagrad_state, edge_count, lhs_owner, lhs_row, rhs_owner, rhs_row, neg_owner, neg_row):
    left_ids = (lhs_owner[..., 0] * ROWS_DEV + lhs_row).reshape(-1, CE).astype(jnp.int32)
    right_ids = (rhs_owner[..., 0] * ROWS_DEV + rhs_row).reshape(-1, CE).astype(jnp.int32)
    neg_ids = (neg_owner[..., 0] * ROWS_DEV + neg_row).reshape(-1, NEG).astype(jnp.int32)
    group_ids = jnp.arange(N_DOM * SLOTS, dtype=jnp.int32)
    bucket = group_ids // SLOTS
    slot_ids = group_ids % SLOTS
    limits = jnp.clip(edge_count[bucket] - slot_ids * CE, 0, CE).astype(jnp.int32)
    row_table = embeddings.astype(jnp.bfloat16)

    def accumulate(gradients, pieces):
        left_now, right_now, neg_now, limit_now = pieces

        def compute(current):
            grad_left, grad_right, grad_shared = group_gradients(row_table[left_now], row_table[right_now], row_table[neg_now], limit_now)
            current = current.at[left_now].add(grad_left.astype(jnp.float32))
            current = current.at[right_now].add(grad_right.astype(jnp.float32))
            current = current.at[neg_now].add(grad_shared.astype(jnp.float32))
            return current

        def keep(current):
            return current
        return (lax.cond(limit_now > 0, compute, keep, gradients), None)
    start = jnp.zeros(embeddings.shape, jnp.float32)
    gradients, unused = lax.scan(accumulate, start, (left_ids, right_ids, neg_ids, limits))
    new_state = adagrad_state + lax.optimization_barrier(jnp.mean(gradients * gradients, axis=1))
    new_embeddings = embeddings - learn_rate * gradients / (jnp.sqrt(new_state)[:, None] + adagrad_eps)
    return (new_embeddings, new_state)
```

```python
from functools import partial

import jax
import jax.numpy as jnp
from jax import lax
from jax.experimental import pallas as pl
from jax.experimental.pallas import tpu as pltpu
from jax.sharding import PartitionSpec as P

learn_rate = 0.1
adagrad_eps = 1e-06
lanes = 128
batch = 4
in_vmem = pl.BlockSpec(memory_space=pltpu.VMEM)
in_smem = pl.BlockSpec(memory_space=pltpu.SMEM)
by_rows = (((1,), (1,)), ((), ()))
f32, bf16, i32 = jnp.float32, jnp.bfloat16, jnp.int32


def params(mib):
    return pltpu.CompilerParams(vmem_limit_bytes=mib * 2**20)


def mul(a, b):
    return jnp.dot(a, b, preferred_element_type=f32)


def mul_t(a, b):
    return lax.dot_general(a, b, by_rows, preferred_element_type=f32)


def iota(shape, dim):
    return lax.broadcasted_iota(i32, shape, dim)


def prep_kernel(rows_dev, limit_ref, *refs):
    index_refs, (ask_ref, spot_ref, fill_ref) = refs[:6], refs[6:]
    peers, stride = ask_ref.shape
    cap = stride // 3
    count = index_refs[0].shape[1]
    part = min(256, count)
    upper = (iota((part, part), 0) < iota((part, part), 1)).astype(f32).astype(bf16)
    peer_of = iota((peers, count), 0)
    slot_of = iota((stride, count), 0)
    spot_ref[...] = jnp.zeros(spot_ref.shape, f32)
    high = low = there = jnp.zeros((peers, stride), f32)
    for kind in range(3):
        owner = index_refs[2 * kind][...]
        row = index_refs[2 * kind + 1][...]
        match = (owner == peer_of).astype(f32)
        seen = jnp.zeros((peers, 1), f32)
        ranks = []
        for start in range(0, count, part):
            now = match[:, start : start + part]
            before = mul(now.astype(bf16), upper) + seen
            seen = seen + jnp.sum(now, axis=1, keepdims=True)
            ranks.append(jnp.sum(now * before, axis=0, keepdims=True))
        rank = jnp.concatenate(ranks, axis=1)
        spot_ref[kind : kind + 1, :] = owner.astype(f32) * cap + rank
        slot = (rank.astype(i32) + kind * cap == slot_of).astype(f32)
        match = match.astype(bf16)
        high += mul_t(match, (slot * (row // 64).astype(f32)).astype(bf16))
        low += mul_t(match, (slot * (row % 64).astype(f32)).astype(bf16))
        there += mul_t(match, slot.astype(bf16))
    asked = (high * 64.0 + low).astype(i32)
    asked = jnp.where(there > 0.5, asked, rows_dev)
    ask_ref[...] = jnp.where(limit_ref[0] > 0, asked, -1)
    place = iota((peers, fill_ref.shape[1]), 1) - iota((peers, fill_ref.shape[1]), 0) * cap
    filled = (place >= 0) & (place.astype(f32) < seen)
    fill_ref[...] = jnp.broadcast_to(
        jnp.sum(filled.astype(f32), axis=0, keepdims=True), fill_ref.shape
    )


def prep(limit, indices, peers, cap, rows_dev):
    count = indices[0].shape[1]
    return pl.pallas_call(
        partial(prep_kernel, rows_dev),
        out_shape=(
            jax.ShapeDtypeStruct((peers, 3 * cap), i32),
            jax.ShapeDtypeStruct((8, count), f32),
            jax.ShapeDtypeStruct((8, peers * cap), f32),
        ),
        in_specs=[in_smem] + [in_vmem] * 6,
        out_specs=(in_vmem,) * 3,
        compiler_params=params(32),
        name="prep",
    )(limit, *indices)


def pack_active(asked_s, asked_v, who, packed):
    peers, stride = asked_v.shape
    packed[...] = jnp.full(packed.shape, -1, i32)

    def step(peer, used):
        active = asked_s[peer, 0] >= 0

        @pl.when(active)
        def take():
            who[used] = peer
            packed[used // batch, pl.ds(used % batch, 1), :stride] = asked_v[pl.ds(peer, 1), :]

        return used + active.astype(i32)

    return lax.fori_loop(0, peers, step, 0)


def fetch_kernel(asked_s, asked_v, table_ref, out_ref, who, packed):
    stride = asked_v.shape[1]
    wide = packed.shape[2]
    rows_dev = table_ref.shape[0]
    used = pack_active(asked_s, asked_v, who, packed)
    row_of = iota((wide, rows_dev), 1)

    def block(number, carry):
        columns = jnp.transpose(packed[number])
        picker = jnp.concatenate(
            [
                (columns[:, j : j + 1] == row_of).astype(f32).astype(bf16)
                for j in range(batch)
            ],
            axis=0,
        )
        rows = mul(picker, table_ref[...])
        for j in range(batch):

            @pl.when(number * batch + j < used)
            def put():
                out_ref[who[number * batch + j]] = rows[j * wide : j * wide + stride].astype(bf16)

        return carry

    lax.fori_loop(0, pl.cdiv(used, batch), block, 0)


def active_scratch(peers, stride):
    wide = pl.cdiv(stride, lanes) * lanes
    return [
        pltpu.SMEM((peers,), i32),
        pltpu.VMEM((pl.cdiv(peers, batch), 8, wide), i32),
    ]


def fetch(asked, table):
    peers, stride = asked.shape
    return pl.pallas_call(
        fetch_kernel,
        out_shape=jax.ShapeDtypeStruct((peers, stride, table.shape[1]), bf16),
        in_specs=[in_smem, in_vmem, in_vmem],
        out_specs=in_vmem,
        scratch_shapes=active_scratch(peers, stride),
        compiler_params=params(40),
        name="fetch",
    )(asked, asked, table)


def train_kernel(
    limit_ref, spot_ref, fill_ref, come_ref, go_ref, wide_ref, place_ref, left_ref, right_ref,
    gl_ref, pg_ref, ps_ref, pr_ref
):
    peers, stride, features = come_ref.shape
    cap = stride // 3
    slots = peers * cap
    count = spot_ref.shape[1]
    part = min(256, count)
    limit = limit_ref[0]

    @pl.when(limit > 0)
    def active():
        def split(peer, carry):
            rows = come_ref[peer].astype(f32)
            for kind in range(3):
                wide_ref[kind, pl.ds(pl.multiple_of(peer * cap, 8), cap), :] = rows[
                    kind * cap : kind * cap + cap
                ]
            return carry

        lax.fori_loop(0, peers, split, 0)
        spot_rows = spot_ref[...]
        spot_columns = jnp.transpose(spot_rows)
        slot_across = iota((part, slots), 1).astype(f32)
        for kind, target in ((0, left_ref), (1, right_ref)):
            held = wide_ref[kind].astype(bf16)
            for start in range(0, count, part):
                column = spot_columns[start : start + part, kind : kind + 1]
                picker = (column == slot_across).astype(f32).astype(bf16)
                target[start : start + part, :] = mul(picker, held).astype(bf16)
        shared_rows = wide_ref[2].astype(bf16)
        fill = fill_ref[0:1, :]
        off_diagonal = (iota((part, part), 0) != iota((part, part), 1)).astype(f32)
        for start in range(0, count, part):
            here = slice(start, start + part)
            left = left_ref[here, :]
            left_wide = left.astype(f32)
            right_wide = right_ref[here, :].astype(f32)
            pos_exp = jnp.exp(jnp.sum(left_wide * right_wide, axis=1, keepdims=True))
            shared_exp = jnp.exp(mul_t(left, shared_rows)) * fill
            total = pos_exp + jnp.sum(shared_exp, axis=1, keepdims=True)
            chunk_exps = []
            for other in range(0, count, part):
                chunk_exp = jnp.exp(mul_t(left, right_ref[other : other + part, :]))
                chunk_exp = chunk_exp * (iota((1, part), 1) + other < limit).astype(f32)
                if other == start:
                    chunk_exp = chunk_exp * off_diagonal
                total = total + jnp.sum(chunk_exp, axis=1, keepdims=True)
                chunk_exps.append(chunk_exp)
            live = (iota((part, 1), 0) + start < limit).astype(f32)
            weight = live / total
            pos_grad = live * (pos_exp / total - 1.0)
            shared_prob = (shared_exp * weight).astype(bf16)
            ps_ref[here, :] = shared_prob
            grad = pos_grad * right_wide + mul(shared_prob, shared_rows)
            for other, chunk_exp in zip(range(0, count, part), chunk_exps):
                chunk_prob = (chunk_exp * weight).astype(bf16)
                pr_ref[here, other : other + part] = chunk_prob
                grad = grad + mul(chunk_prob, right_ref[other : other + part, :])
            gl_ref[here, :] = grad.astype(bf16)
            pg_ref[here, :] = pos_grad * left_wide
        left_turned = jnp.transpose(left_ref[...].astype(f32)).astype(bf16)
        place_ref[2] = jnp.transpose(mul(left_turned, ps_ref[...]))
        grad_right = jnp.transpose(mul(left_turned, pr_ref[...])) + pg_ref[...]
        right_ref[...] = grad_right.astype(bf16)
        slot_down = iota((part, count), 0).astype(f32)
        for kind, source in ((0, gl_ref), (1, right_ref)):
            for start in range(0, slots, part):
                picker = (spot_rows[kind : kind + 1, :] - float(start) == slot_down)
                picker = picker.astype(f32).astype(bf16)
                place_ref[kind, start : start + part, :] = mul(picker, source[...])

        def join(peer, carry):
            go_ref[peer] = jnp.concatenate(
                [
                    place_ref[kind, pl.ds(pl.multiple_of(peer * cap, 8), cap), :]
                    for kind in range(3)
                ],
                axis=0,
            ).astype(bf16)
            return carry

        lax.fori_loop(0, peers, join, 0)


def train(limit, spots, fill, arrived):
    peers, stride, features = arrived.shape
    count = spots.shape[1]
    slots = fill.shape[1]
    return pl.pallas_call(
        train_kernel,
        out_shape=jax.ShapeDtypeStruct(arrived.shape, bf16),
        in_specs=[in_smem, in_vmem, in_vmem, in_vmem],
        out_specs=in_vmem,
        scratch_shapes=[
            pltpu.VMEM((3, slots, features), f32),
            pltpu.VMEM((3, slots, features), f32),
            pltpu.VMEM((count, features), bf16),
            pltpu.VMEM((count, features), bf16),
            pltpu.VMEM((count, features), bf16),
            pltpu.VMEM((count, features), f32),
            pltpu.VMEM((count, slots), bf16),
            pltpu.VMEM((count, count), bf16),
        ],
        compiler_params=params(48),
        name="train",
    )(limit, spots, fill, arrived)


def update_kernel(
    asked_s, asked_v, back_ref, table_ref, state_ref, out_ref, new_state_ref, who, packed, held,
    turned, turned_new
):
    peers, stride = asked_v.shape
    wide = packed.shape[2]
    rows_dev, features = table_ref.shape
    total_blocks = pl.cdiv(peers, batch)
    part = min(512, rows_dev)
    per_part = part // lanes
    used = pack_active(asked_s, asked_v, who, packed)
    blocks = pl.cdiv(used, batch)

    def take(number, carry):
        place = pl.ds(pl.multiple_of(number * wide, wide), wide)

        @pl.when(number < used)
        def full():
            rows = back_ref[who[number]].astype(f32)
            if wide > stride:
                rows = jnp.concatenate([rows, jnp.zeros((wide - stride, features), f32)], axis=0)
            held[place, :] = rows.astype(bf16)

        @pl.when(number >= used)
        def empty():
            held[place, :] = jnp.zeros((wide, features), bf16)

        return carry

    lax.fori_loop(0, total_blocks * batch, take, 0)
    state_turned = jnp.transpose(state_ref[...])
    for number in range(rows_dev // part):
        turned[number, :, :per_part] = state_turned[:, number * per_part : (number + 1) * per_part]

    def finish(number, gradients):
        states = turned[number]
        for j in range(per_part):
            grads = gradients[j * lanes : (j + 1) * lanes]
            state = states[:, j : j + 1] + jnp.mean(grads * grads, axis=1, keepdims=True)
            turned_new[number, :, j : j + 1] = state
            place = pl.ds(pl.multiple_of(number * part + j * lanes, lanes), lanes)
            out_ref[place, :] = table_ref[place, :] - learn_rate * grads / (
                jnp.sqrt(state) + adagrad_eps
            )

    def with_blocks(take_blocks):
        def one_part(number, carry):
            row_of = iota((part, wide), 0) + number * part
            picker = jnp.concatenate(
                [
                    (packed[k // batch, k % batch : k % batch + 1, :] == row_of)
                    .astype(f32)
                    .astype(bf16)
                    for k in range(take_blocks * batch)
                ],
                axis=1,
            )
            finish(number, mul(picker, held[: take_blocks * batch * wide, :]))
            return carry

        lax.fori_loop(0, rows_dev // part, one_part, 0)

    first = max(1, total_blocks // 2)
    for take_blocks in range(first, total_blocks + 1):
        chosen = blocks <= first if take_blocks == first else blocks == take_blocks
        pl.when(chosen)(partial(with_blocks, take_blocks))

    for number in range(rows_dev // part):
        new_state_ref[number * per_part : (number + 1) * per_part, :] = jnp.transpose(
            turned_new[number]
        )[:per_part]


def update(asked, returned, table, state):
    peers, stride = asked.shape
    rows_dev, features = table.shape
    wide = pl.cdiv(stride, lanes) * lanes
    part = min(512, rows_dev)
    kept = pl.cdiv(peers, batch) * batch * wide
    new_table, new_state = pl.pallas_call(
        update_kernel,
        out_shape=(
            jax.ShapeDtypeStruct(table.shape, f32),
            jax.ShapeDtypeStruct((rows_dev // lanes, lanes), f32),
        ),
        in_specs=[in_smem, in_vmem, in_vmem, in_vmem, in_vmem],
        out_specs=(in_vmem, in_vmem),
        scratch_shapes=active_scratch(peers, stride)
        + [
            pltpu.VMEM((kept, features), bf16),
            pltpu.VMEM((rows_dev // part, lanes, lanes), f32),
            pltpu.VMEM((rows_dev // part, lanes, lanes), f32),
        ],
        compiler_params=params(48),
        name="update",
    )(asked, asked, returned, table, state.reshape(rows_dev // lanes, lanes))
    return new_table, new_state.reshape(rows_dev)


def body(
    embeddings,
    adagrad_state,
    edge_count,
    lhs_owner,
    lhs_row,
    rhs_owner,
    rhs_row,
    neg_owner,
    neg_row,
):
    axes = ("dom", "group")
    rows_dev = embeddings.shape[0]
    group_len = lhs_row.shape[2]
    peers = lax.axis_size("dom") * lax.axis_size("group")
    cap = pl.cdiv(5 * group_len // (4 * peers), 8) * 8
    limit = jnp.clip(edge_count - lax.axis_index("group") * group_len, 0, group_len)
    indices = [
        x.reshape(1, group_len)
        for x in (lhs_owner, lhs_row, rhs_owner, rhs_row, neg_owner, neg_row)
    ]
    ask, spots, fill = prep(limit, indices, peers, cap, rows_dev)
    asked = lax.all_to_all(ask, axes, split_axis=0, concat_axis=0, tiled=True)
    answer = fetch(asked, embeddings.astype(bf16))
    arrived = lax.all_to_all(answer, axes, split_axis=0, concat_axis=0, tiled=True)
    grads = train(limit, spots, fill, arrived)
    returned = lax.all_to_all(grads, axes, split_axis=0, concat_axis=0, tiled=True)
    return update(asked, returned, embeddings, adagrad_state)


def solution(mesh):
    return jax.shard_map(
        body,
        mesh=mesh,
        in_specs=(
            P(("dom", "group"), None),
            P(("dom", "group")),
            P("dom"),
            P("dom", "group", None, None),
            P("dom", "group", None),
            P("dom", "group", None, None),
            P("dom", "group", None),
            P("dom", "group", None, None),
            P("dom", "group", None),
        ),
        out_specs=(P(("dom", "group"), None), P(("dom", "group"))),
        check_vma=False,
    )
```

```python
from functools import partial

import jax
import jax.numpy as jnp
from jax import lax
from jax.experimental import pallas as pl
from jax.experimental.pallas import tpu as pltpu
from jax.sharding import PartitionSpec as P

learn_rate = 0.1
adagrad_eps = 1e-06
lanes = 128
batch = 4
in_vmem = pl.BlockSpec(memory_space=pltpu.VMEM)
in_smem = pl.BlockSpec(memory_space=pltpu.SMEM)
by_rows = (((1,), (1,)), ((), ()))
f32, bf16, i32 = jnp.float32, jnp.bfloat16, jnp.int32


def params(mib):
    return pltpu.CompilerParams(vmem_limit_bytes=mib * 2**20)


def mul(a, b):
    return jnp.dot(a, b, preferred_element_type=f32)


def mul_t(a, b):
    return lax.dot_general(a, b, by_rows, preferred_element_type=f32)


def iota(shape, dim):
    return lax.broadcasted_iota(i32, shape, dim)


def prep_kernel(
    rows_dev, count_hbm, *refs
):
    index_hbm, (ask_ref, spot_ref, fill_ref, limit_ref) = refs[:6], refs[6:10]
    index_refs, edges, arrivals = refs[10:16], refs[16], refs[17]
    copies = [
        pltpu.make_async_copy(source, target, arrivals.at[number])
        for number, (source, target) in enumerate(
            zip((count_hbm, *index_hbm), (edges, *index_refs))
        )
    ]
    for copy in copies:
        copy.start()
    peers, stride = ask_ref.shape
    cap = stride // 3
    count = index_refs[0].shape[1]
    part = min(256, count)
    upper = (iota((part, part), 0) < iota((part, part), 1)).astype(f32).astype(bf16)
    peer_of = iota((peers, count), 0)
    slot_of = iota((stride, count), 0)
    spot_ref[...] = jnp.zeros(spot_ref.shape, f32)
    high = low = there = jnp.zeros((peers, stride), f32)
    for copy in copies:
        copy.wait()
    limit = jnp.clip(edges[0] - lax.axis_index("group") * count, 0, count)
    limit_ref[0] = limit
    for kind in range(3):
        owner = index_refs[2 * kind][...]
        row = index_refs[2 * kind + 1][...]
        match = (owner == peer_of).astype(f32)
        seen = jnp.zeros((peers, 1), f32)
        ranks = []
        for start in range(0, count, part):
            now = match[:, start : start + part]
            before = mul(now.astype(bf16), upper) + seen
            seen = seen + jnp.sum(now, axis=1, keepdims=True)
            ranks.append(jnp.sum(now * before, axis=0, keepdims=True))
        rank = jnp.concatenate(ranks, axis=1)
        spot_ref[kind : kind + 1, :] = owner.astype(f32) * cap + rank
        slot = (rank.astype(i32) + kind * cap == slot_of).astype(f32)
        match = match.astype(bf16)
        high += mul_t(match, (slot * (row // 64).astype(f32)).astype(bf16))
        low += mul_t(match, (slot * (row % 64).astype(f32)).astype(bf16))
        there += mul_t(match, slot.astype(bf16))
    asked = (high * 64.0 + low).astype(i32)
    asked = jnp.where(there > 0.5, asked, rows_dev)
    ask_ref[...] = jnp.where(limit > 0, asked, -1)
    place = iota((peers, fill_ref.shape[1]), 1) - iota((peers, fill_ref.shape[1]), 0) * cap
    filled = (place >= 0) & (place.astype(f32) < seen)
    fill_ref[...] = jnp.broadcast_to(
        jnp.sum(filled.astype(f32), axis=0, keepdims=True), fill_ref.shape
    )


def prep(edge_count, indices, peers, cap, rows_dev):
    count = indices[0].shape[1]
    anywhere = pl.BlockSpec(memory_space=pl.ANY)
    return pl.pallas_call(
        partial(prep_kernel, rows_dev),
        out_shape=(
            jax.ShapeDtypeStruct((peers, 3 * cap), i32),
            jax.ShapeDtypeStruct((8, count), f32),
            jax.ShapeDtypeStruct((8, peers * cap), f32),
            jax.ShapeDtypeStruct((1,), i32),
        ),
        in_specs=[anywhere] * 7,
        out_specs=(in_vmem, in_vmem, in_vmem, in_smem),
        scratch_shapes=[pltpu.VMEM((1, count), i32)] * 6
        + [pltpu.SMEM((1,), i32), pltpu.SemaphoreType.DMA((7,))],
        compiler_params=params(32),
        name="prep",
    )(edge_count, *indices)


def pack_active(asked_s, asked_v, who, packed):
    peers, stride = asked_v.shape
    packed[...] = jnp.full(packed.shape, -1, i32)
    used = 0
    for peer in range(peers):
        who[used] = peer
        packed[pl.ds(used, 1), :stride] = asked_v[peer : peer + 1, :]
        used = used + (asked_s[peer, 0] >= 0).astype(i32)
    packed[pl.ds(used, 1), :] = jnp.full((1, packed.shape[1]), -1, i32)
    return used


def fetch_kernel(asked_s, asked_v, table_ref, out_ref, who, packed):
    stride = asked_v.shape[1]
    wide = packed.shape[1]
    rows_dev = table_ref.shape[0]
    used = pack_active(asked_s, asked_v, who, packed)
    row_of = iota((wide, rows_dev), 1)

    def block(first, size):
        columns = jnp.transpose(packed[pl.ds(pl.multiple_of(first, 8), 8), :])
        picker = jnp.concatenate(
            [(columns[:, j : j + 1] == row_of).astype(f32).astype(bf16) for j in range(size)],
            axis=0,
        )
        rows = mul(picker, table_ref[...])
        for j in range(size):

            @pl.when(first + j < used)
            def put():
                out_ref[who[first + j]] = rows[j * wide : j * wide + stride].astype(bf16)

    rest = used % 8
    large = used // 8 + (rest > 4).astype(i32)
    lax.fori_loop(0, large, lambda number, carry: (block(number * 8, 8), carry)[1], 0)
    pl.when((rest > 0) & (rest <= 4))(lambda: block(large * 8, 4))


def active_scratch(peers, stride):
    wide = pl.cdiv(stride, lanes) * lanes
    return [pltpu.SMEM((peers + 8,), i32), pltpu.VMEM((pl.cdiv(peers, 8) * 8 + 8, wide), i32)]


def fetch(asked, table):
    peers, stride = asked.shape
    return pl.pallas_call(
        fetch_kernel,
        out_shape=jax.ShapeDtypeStruct((peers, stride, table.shape[1]), bf16),
        in_specs=[in_smem, in_vmem, in_vmem],
        out_specs=in_vmem,
        scratch_shapes=active_scratch(peers, stride),
        compiler_params=params(40),
        name="fetch",
    )(asked, asked, table)


def train_kernel(
    limit_ref, spot_ref, fill_ref, come_ref, go_ref, wide_ref, place_ref, left_ref, right_ref,
    gl_ref, pg_ref, ps_ref, pr_ref
):
    peers, stride, features = come_ref.shape
    cap = stride // 3
    slots = peers * cap
    count = spot_ref.shape[1]
    part = min(256, count)
    limit = limit_ref[0]

    @pl.when(limit > 0)
    def active():
        def split(peer, carry):
            rows = come_ref[peer].astype(f32)
            for kind in range(3):
                wide_ref[kind, pl.ds(pl.multiple_of(peer * cap, 8), cap), :] = rows[
                    kind * cap : kind * cap + cap
                ]
            return carry

        lax.fori_loop(0, peers, split, 0)
        spot_rows = spot_ref[...]
        spot_columns = jnp.transpose(spot_rows)
        slot_across = iota((part, slots), 1).astype(f32)
        for kind, target in ((0, left_ref), (1, right_ref)):
            held = wide_ref[kind].astype(bf16)
            for start in range(0, count, part):
                column = spot_columns[start : start + part, kind : kind + 1]
                picker = (column == slot_across).astype(f32).astype(bf16)
                target[start : start + part, :] = mul(picker, held).astype(bf16)
        shared_rows = wide_ref[2].astype(bf16)
        fill = fill_ref[0:1, :]
        off_diagonal = (iota((part, part), 0) != iota((part, part), 1)).astype(f32)
        for start in range(0, count, part):
            here = slice(start, start + part)
            left = left_ref[here, :]
            left_wide = left.astype(f32)
            right_wide = right_ref[here, :].astype(f32)
            pos_exp = jnp.exp(jnp.sum(left_wide * right_wide, axis=1, keepdims=True))
            shared_exp = jnp.exp(mul_t(left, shared_rows)) * fill
            total = pos_exp + jnp.sum(shared_exp, axis=1, keepdims=True)
            chunk_exps = []
            for other in range(0, count, part):
                chunk_exp = jnp.exp(mul_t(left, right_ref[other : other + part, :]))
                chunk_exp = chunk_exp * (iota((1, part), 1) + other < limit).astype(f32)
                if other == start:
                    chunk_exp = chunk_exp * off_diagonal
                total = total + jnp.sum(chunk_exp, axis=1, keepdims=True)
                chunk_exps.append(chunk_exp)
            live = (iota((part, 1), 0) + start < limit).astype(f32)
            weight = live / total
            pos_grad = live * (pos_exp / total - 1.0)
            shared_prob = (shared_exp * weight).astype(bf16)
            ps_ref[here, :] = shared_prob
            grad = pos_grad * right_wide + mul(shared_prob, shared_rows)
            for other, chunk_exp in zip(range(0, count, part), chunk_exps):
                chunk_prob = (chunk_exp * weight).astype(bf16)
                pr_ref[here, other : other + part] = chunk_prob
                grad = grad + mul(chunk_prob, right_ref[other : other + part, :])
            gl_ref[here, :] = grad.astype(bf16)
            pg_ref[here, :] = pos_grad * left_wide
        left_turned = jnp.transpose(left_ref[...].astype(f32)).astype(bf16)
        place_ref[2] = jnp.transpose(mul(left_turned, ps_ref[...]))
        grad_right = jnp.transpose(mul(left_turned, pr_ref[...])) + pg_ref[...]
        right_ref[...] = grad_right.astype(bf16)
        slot_down = iota((part, count), 0).astype(f32)
        for kind, source in ((0, gl_ref), (1, right_ref)):
            for start in range(0, slots, part):
                picker = (spot_rows[kind : kind + 1, :] - float(start) == slot_down)
                picker = picker.astype(f32).astype(bf16)
                place_ref[kind, start : start + part, :] = mul(picker, source[...])

        def join(peer, carry):
            go_ref[peer] = jnp.concatenate(
                [
                    place_ref[kind, pl.ds(pl.multiple_of(peer * cap, 8), cap), :]
                    for kind in range(3)
                ],
                axis=0,
            ).astype(bf16)
            return carry

        lax.fori_loop(0, peers, join, 0)


def train(limit, spots, fill, arrived):
    peers, stride, features = arrived.shape
    count = spots.shape[1]
    slots = fill.shape[1]
    return pl.pallas_call(
        train_kernel,
        out_shape=jax.ShapeDtypeStruct(arrived.shape, bf16),
        in_specs=[in_smem, in_vmem, in_vmem, in_vmem],
        out_specs=in_vmem,
        scratch_shapes=[
            pltpu.VMEM((3, slots, features), f32),
            pltpu.VMEM((3, slots, features), f32),
            pltpu.VMEM((count, features), bf16),
            pltpu.VMEM((count, features), bf16),
            pltpu.VMEM((count, features), bf16),
            pltpu.VMEM((count, features), f32),
            pltpu.VMEM((count, slots), bf16),
            pltpu.VMEM((count, count), bf16),
        ],
        compiler_params=params(48),
        name="train",
    )(limit, spots, fill, arrived)


def update_kernel(
    asked_s, asked_v, back_ref, table_ref, state_ref, out_hbm, new_state_ref, who, packed, held,
    turned, turned_new, grads_ref, out_ref, left
):
    peers, stride = asked_v.shape
    wide = packed.shape[1]
    rows_dev, features = table_ref.shape
    total_blocks = pl.cdiv(peers, batch)
    part = min(512, rows_dev)
    parts = rows_dev // part
    per_part = part // lanes
    used = pack_active(asked_s, asked_v, who, packed)
    blocks = pl.cdiv(used, batch)
    if wide > stride:
        tail = stride // 16 * 16
        held[:, tail:, :] = jnp.zeros((held.shape[0], wide - tail, features), bf16)

    def take(number, carry):
        held[number, :stride, :] = back_ref[who[number]]
        return carry

    def clear(number, carry):
        held[number] = jnp.zeros((wide, features), bf16)
        return carry

    lax.fori_loop(0, used, take, 0)
    lax.fori_loop(used, blocks * batch, clear, 0)
    state_turned = jnp.transpose(state_ref[...])
    for number in range(parts):
        turned[number, :, :per_part] = state_turned[:, number * per_part : (number + 1) * per_part]

    def leave(number):
        rows = pl.ds(pl.multiple_of(number * part, part), part)
        return pltpu.make_async_copy(out_ref.at[rows], out_hbm.at[rows], left.at[number])

    def finish(number):
        grads = [grads_ref[j * lanes : (j + 1) * lanes, :] for j in range(per_part)]
        sums = [jnp.sum(g * g, axis=1, keepdims=True) for g in grads]
        state = turned[number, :, :per_part] + jnp.concatenate(sums, axis=1) * (1.0 / features)
        turned_new[number, :, :per_part] = state
        scale = learn_rate / (jnp.sqrt(state) + adagrad_eps)
        for j in range(per_part):
            place = pl.ds(pl.multiple_of(number * part + j * lanes, lanes), lanes)
            out_ref[place, :] = table_ref[place, :] - grads[j] * scale[:, j : j + 1]

    def with_blocks(take_blocks):
        rows_held = held[: take_blocks * batch].reshape(take_blocks * batch * wide, features)

        def gather(number):
            row_of = iota((part, wide), 0) + number * part
            picker = jnp.concatenate(
                [
                    (packed[k : k + 1, :] == row_of).astype(f32).astype(bf16)
                    for k in range(take_blocks * batch)
                ],
                axis=1,
            )
            return mul(picker, rows_held)

        def step(number, carry):
            finish(number - 1)
            grads_ref[...] = gather(number)
            leave(number - 1).start()
            return carry

        grads_ref[...] = gather(0)
        lax.fori_loop(1, parts, step, 0)

    first = max(1, total_blocks // 2)
    for take_blocks in range(first, total_blocks + 1):
        chosen = blocks <= first if take_blocks == first else blocks == take_blocks
        pl.when(chosen)(partial(with_blocks, take_blocks))

    finish(parts - 1)
    leave(parts - 1).start()
    for number in range(parts):
        new_state_ref[number * per_part : (number + 1) * per_part, :] = jnp.transpose(
            turned_new[number]
        )[:per_part]
    for number in range(parts):
        leave(number).wait()


def update(asked, returned, table, state):
    peers, stride = asked.shape
    rows_dev, features = table.shape
    wide = pl.cdiv(stride, lanes) * lanes
    part = min(512, rows_dev)
    parts = rows_dev // part
    new_table, new_state = pl.pallas_call(
        update_kernel,
        out_shape=(
            jax.ShapeDtypeStruct(table.shape, f32),
            jax.ShapeDtypeStruct((rows_dev // lanes, lanes), f32),
        ),
        in_specs=[in_smem, in_vmem, in_vmem, in_vmem, in_vmem],
        out_specs=(pl.BlockSpec(memory_space=pl.ANY), in_vmem),
        scratch_shapes=active_scratch(peers, stride)
        + [
            pltpu.VMEM((pl.cdiv(peers, batch) * batch, wide, features), bf16),
            pltpu.VMEM((parts, lanes, lanes), f32),
            pltpu.VMEM((parts, lanes, lanes), f32),
            pltpu.VMEM((part, features), f32),
            pltpu.VMEM(table.shape, f32),
            pltpu.SemaphoreType.DMA((parts,)),
        ],
        compiler_params=params(48),
        name="update",
    )(asked, asked, returned, table, state.reshape(rows_dev // lanes, lanes))
    return new_table, new_state.reshape(rows_dev)


def body(
    embeddings,
    adagrad_state,
    edge_count,
    lhs_owner,
    lhs_row,
    rhs_owner,
    rhs_row,
    neg_owner,
    neg_row,
):
    axes = ("dom", "group")
    rows_dev = embeddings.shape[0]
    group_len = lhs_row.shape[2]
    peers = lax.axis_size("dom") * lax.axis_size("group")
    cap = pl.cdiv(5 * group_len // (4 * peers), 8) * 8
    indices = [
        x.reshape(1, group_len)
        for x in (lhs_owner, lhs_row, rhs_owner, rhs_row, neg_owner, neg_row)
    ]
    ask, spots, fill, limit = prep(edge_count, indices, peers, cap, rows_dev)
    asked = lax.all_to_all(ask, axes, split_axis=0, concat_axis=0, tiled=True)
    answer = fetch(asked, embeddings.astype(bf16))
    arrived = lax.all_to_all(answer, axes, split_axis=0, concat_axis=0, tiled=True)
    grads = train(limit, spots, fill, arrived)
    returned = lax.all_to_all(grads, axes, split_axis=0, concat_axis=0, tiled=True)
    return update(asked, returned, embeddings, adagrad_state)


def solution(mesh):
    return jax.shard_map(
        body,
        mesh=mesh,
        in_specs=(
            P(("dom", "group"), None),
            P(("dom", "group")),
            P("dom"),
            P("dom", "group", None, None),
            P("dom", "group", None),
            P("dom", "group", None, None),
            P("dom", "group", None),
            P("dom", "group", None, None),
            P("dom", "group", None),
        ),
        out_specs=(P(("dom", "group"), None), P(("dom", "group"))),
        check_vma=False,
    )
```

```python
from functools import partial

import jax
import jax.numpy as jnp
from jax import lax
from jax.experimental import pallas as pl
from jax.experimental.pallas import tpu as pltpu
from jax.sharding import PartitionSpec as P

learn_rate = 0.1
adagrad_eps = 1e-06
lanes = 128
batch = 4
in_vmem = pl.BlockSpec(memory_space=pltpu.VMEM)
in_hbm = pl.BlockSpec(memory_space=pltpu.HBM)
by_rows = (((1,), (1,)), ((), ()))
f32, bf16, i32 = jnp.float32, jnp.bfloat16, jnp.int32


def params(mib):
    return pltpu.CompilerParams(vmem_limit_bytes=mib * 2**20)


def mul(a, b):
    return jnp.dot(a, b, preferred_element_type=f32)


def mul_t(a, b):
    return lax.dot_general(a, b, by_rows, preferred_element_type=f32)


def iota(shape, dim):
    return lax.broadcasted_iota(i32, shape, dim)


def prep_kernel(
    rows_dev, count_hbm, *refs
):
    index_hbm, (ask_ref, spot_ref, fill_ref) = refs[:6], refs[6:9]
    index_refs, edges, arrivals = refs[9:15], refs[15], refs[16]
    copies = [
        pltpu.make_async_copy(source, target, arrivals.at[number])
        for number, (source, target) in enumerate(
            zip((count_hbm, *index_hbm), (edges, *index_refs))
        )
    ]
    for copy in copies:
        copy.start()
    peers, stride = ask_ref.shape
    cap = stride // 3
    count = index_refs[0].shape[1]
    part = min(256, count)
    upper = (iota((part, part), 0) < iota((part, part), 1)).astype(f32).astype(bf16)
    peer_of = iota((peers, count), 0)
    slot_of = iota((stride, count), 0)
    spot_ref[...] = jnp.zeros(spot_ref.shape, f32)
    high = low = there = jnp.zeros((peers, stride), f32)
    for copy in copies:
        copy.wait()
    limit = jnp.clip(edges[0] - lax.axis_index("group") * count, 0, count)
    spot_ref[3:4, :] = jnp.full((1, count), limit, i32).astype(f32)
    for kind in range(3):
        owner = index_refs[2 * kind][...]
        row = index_refs[2 * kind + 1][...]
        match = (owner == peer_of).astype(f32)
        seen = jnp.zeros((peers, 1), f32)
        ranks = []
        for start in range(0, count, part):
            now = match[:, start : start + part]
            before = mul(now.astype(bf16), upper) + seen
            seen = seen + jnp.sum(now, axis=1, keepdims=True)
            ranks.append(jnp.sum(now * before, axis=0, keepdims=True))
        rank = jnp.concatenate(ranks, axis=1)
        spot_ref[kind : kind + 1, :] = owner.astype(f32) * cap + rank
        slot = (rank.astype(i32) + kind * cap == slot_of).astype(f32)
        match = match.astype(bf16)
        high += mul_t(match, (slot * (row // 64).astype(f32)).astype(bf16))
        low += mul_t(match, (slot * (row % 64).astype(f32)).astype(bf16))
        there += mul_t(match, slot.astype(bf16))
    asked = (high * 64.0 + low).astype(i32)
    asked = jnp.where(there > 0.5, asked, rows_dev)
    ask_ref[...] = jnp.where(limit > 0, asked, -1)
    place = iota((peers, fill_ref.shape[1]), 1) - iota((peers, fill_ref.shape[1]), 0) * cap
    filled = (place >= 0) & (place.astype(f32) < seen)
    fill_ref[...] = jnp.broadcast_to(
        jnp.sum(filled.astype(f32), axis=0, keepdims=True), fill_ref.shape
    )


def prep(edge_count, indices, peers, cap, rows_dev):
    count = indices[0].shape[1]
    return pl.pallas_call(
        partial(prep_kernel, rows_dev),
        out_shape=(
            jax.ShapeDtypeStruct((peers, 3 * cap), i32),
            jax.ShapeDtypeStruct((8, count), f32),
            jax.ShapeDtypeStruct((8, peers * cap), f32),
        ),
        in_specs=[in_hbm] * 7,
        out_specs=(in_vmem, in_vmem, in_vmem),
        scratch_shapes=[pltpu.VMEM((1, count), i32)] * 6
        + [pltpu.SMEM((1,), i32), pltpu.SemaphoreType.DMA((7,))],
        compiler_params=params(62),
        name="prep",
    )(edge_count, *indices)


def pack_active(asked_ref, who, packed):
    peers, stride = asked_ref.shape
    bits = 16
    flags = (asked_ref[:, 0:1] >= 0).astype(f32)
    flags = flags * (1 << iota((peers, 1), 0) % bits).astype(f32)
    words = [jnp.sum(flags[k : k + bits]).astype(i32) for k in range(0, peers, bits)]
    packed[...] = jnp.full(packed.shape, -1, i32)
    used = 0
    for peer in range(peers):
        who[used] = peer
        packed[pl.ds(used, 1), :stride] = asked_ref[peer : peer + 1, :]
        used = used + ((words[peer // bits] >> (peer % bits)) & 1)
    packed[pl.ds(used, 1), :] = jnp.full((1, packed.shape[1]), -1, i32)
    return used


def fetch_kernel(asked_ref, table_ref, out_ref, who, packed):
    stride = asked_ref.shape[1]
    wide = packed.shape[1]
    rows_dev = table_ref.shape[0]
    used = pack_active(asked_ref, who, packed)
    row_of = iota((wide, rows_dev), 1)

    def block(first, size):
        columns = jnp.transpose(packed[pl.ds(pl.multiple_of(first, 8), 8), :])
        picker = jnp.concatenate(
            [(columns[:, j : j + 1] == row_of).astype(f32).astype(bf16) for j in range(size)],
            axis=0,
        )
        rows = mul(picker, table_ref[...])
        for j in range(size):

            @pl.when(first + j < used)
            def put():
                out_ref[who[first + j]] = rows[j * wide : j * wide + stride].astype(bf16)

    rest = used % 8
    large = used // 8 + (rest > 4).astype(i32)
    lax.fori_loop(0, large, lambda number, carry: (block(number * 8, 8), carry)[1], 0)
    pl.when((rest > 0) & (rest <= 4))(lambda: block(large * 8, 4))


def active_scratch(peers, stride):
    wide = pl.cdiv(stride, lanes) * lanes
    return [pltpu.SMEM((peers + 8,), i32), pltpu.VMEM((pl.cdiv(peers, 8) * 8 + 8, wide), i32)]


def fetch(asked, table):
    peers, stride = asked.shape
    return pl.pallas_call(
        fetch_kernel,
        out_shape=jax.ShapeDtypeStruct((peers, stride, table.shape[1]), bf16),
        in_specs=[in_vmem, in_vmem],
        out_specs=in_vmem,
        scratch_shapes=active_scratch(peers, stride),
        compiler_params=params(40),
        name="fetch",
    )(asked, table)


def train_kernel(
    spot_ref, fill_ref, come_ref, go_ref, wide_ref, place_ref, left_ref, right_ref, live_ref,
    gl_ref, pg_ref, ps_ref, pr_ref
):
    peers, stride, features = come_ref.shape
    cap = stride // 3
    slots = peers * cap
    count = spot_ref.shape[1]
    part = min(256, count)
    starts = range(0, count, part)
    for peer in range(peers):
        rows = come_ref[peer].astype(f32)
        for kind in range(3):
            wide_ref[kind, peer * cap : peer * cap + cap, :] = rows[kind * cap : kind * cap + cap]
    spot_rows = spot_ref[...]
    spot_columns = jnp.transpose(spot_rows)
    limit = spot_rows[3:4, 0:1]
    live_across = (iota((1, count), 1).astype(f32) < limit).astype(f32)
    live_down = (iota((count, 1), 0).astype(f32) < limit).astype(f32)
    slot_across = iota((part, slots), 1).astype(f32)
    for kind, target in ((0, left_ref), (1, right_ref)):
        held = wide_ref[kind].astype(bf16)
        for start in starts:
            column = spot_columns[start : start + part, kind : kind + 1]
            picker = (column == slot_across).astype(f32).astype(bf16)
            rows = mul(picker, held)
            target[start : start + part, :] = rows.astype(bf16)
            if kind == 1:
                rows = rows * live_down[start : start + part]
                live_ref[start : start + part, :] = rows.astype(bf16)
    shared_rows = wide_ref[2].astype(bf16)
    fill = fill_ref[0:1, :]
    off_diagonal = (iota((part, part), 0) != iota((part, part), 1)).astype(f32)
    for start in starts:
        here = slice(start, start + part)
        left = left_ref[here, :]
        left_wide = left.astype(f32)
        right_wide = right_ref[here, :].astype(f32)
        pos_exp = jnp.exp(jnp.sum(left_wide * right_wide, axis=1, keepdims=True))
        shared_exp = jnp.exp(mul_t(left, shared_rows))
        total = pos_exp + jnp.sum(shared_exp * fill, axis=1, keepdims=True)
        chunk_exps = []
        for other in starts:
            chunk_exp = jnp.exp(mul_t(left, right_ref[other : other + part, :]))
            if other == start:
                chunk_exp = chunk_exp * off_diagonal
            counted = chunk_exp * live_across[:, other : other + part]
            total = total + jnp.sum(counted, axis=1, keepdims=True)
            chunk_exps.append(chunk_exp)
        live = live_down[here]
        weight = live / total
        pos_grad = live * (pos_exp / total - 1.0)
        ps_ref[here, :] = (shared_exp * weight).astype(bf16)
        for other, chunk_exp in zip(starts, chunk_exps):
            pr_ref[here, other : other + part] = (chunk_exp * weight).astype(bf16)
        pull = mul(ps_ref[here, :], shared_rows) + mul(pr_ref[here, :], live_ref[...])
        gl_ref[here, :] = (pos_grad * right_wide + pull).astype(bf16)
        pg_ref[here, :] = pos_grad * left_wide
    left_turned = jnp.transpose(left_ref[...].astype(f32)).astype(bf16)
    place_ref[2] = jnp.transpose(mul(left_turned, ps_ref[...]))
    grad_right = jnp.transpose(mul(left_turned, pr_ref[...])) * live_down + pg_ref[...]
    right_ref[...] = grad_right.astype(bf16)
    slot_down = iota((part, count), 0).astype(f32)
    for kind, source in ((0, gl_ref), (1, right_ref)):
        for start in range(0, slots, part):
            picker = spot_rows[kind : kind + 1, :] - float(start) == slot_down
            picker = picker.astype(f32).astype(bf16)
            place_ref[kind, start : start + part, :] = mul(picker, source[...])
    for peer in range(peers):
        rows = [place_ref[kind, peer * cap : peer * cap + cap, :] for kind in range(3)]
        go_ref[peer] = jnp.concatenate(rows, axis=0).astype(bf16)


def train(spots, fill, arrived):
    peers, stride, features = arrived.shape
    count = spots.shape[1]
    slots = fill.shape[1]
    return pl.pallas_call(
        train_kernel,
        out_shape=jax.ShapeDtypeStruct(arrived.shape, bf16),
        in_specs=[in_vmem, in_vmem, in_vmem],
        out_specs=in_vmem,
        scratch_shapes=[
            pltpu.VMEM((3, slots, features), f32),
            pltpu.VMEM((3, slots, features), f32),
            pltpu.VMEM((count, features), bf16),
            pltpu.VMEM((count, features), bf16),
            pltpu.VMEM((count, features), bf16),
            pltpu.VMEM((count, features), bf16),
            pltpu.VMEM((count, features), f32),
            pltpu.VMEM((count, slots), bf16),
            pltpu.VMEM((count, count), bf16),
        ],
        compiler_params=params(48),
        name="train",
    )(spots, fill, arrived)


def update_kernel(
    asked_ref, back_ref, table_ref, state_ref, out_hbm, new_state_ref, who, packed, held,
    turned, turned_new, grads_ref, out_ref, left
):
    peers, stride = asked_ref.shape
    wide = packed.shape[1]
    rows_dev, features = table_ref.shape
    total_blocks = pl.cdiv(peers, batch)
    part = min(512, rows_dev)
    parts = rows_dev // part
    per_part = part // lanes
    used = pack_active(asked_ref, who, packed)
    blocks = pl.cdiv(used, batch)
    if wide > stride:
        tail = stride // 16 * 16
        held[:, tail:, :] = jnp.zeros((held.shape[0], wide - tail, features), bf16)

    def take(number, carry):
        held[number, :stride, :] = back_ref[who[number]]
        return carry

    def clear(number, carry):
        held[number] = jnp.zeros((wide, features), bf16)
        return carry

    lax.fori_loop(0, used, take, 0)
    lax.fori_loop(used, blocks * batch, clear, 0)
    state_turned = jnp.transpose(state_ref[...])
    for number in range(parts):
        turned[number, :, :per_part] = state_turned[:, number * per_part : (number + 1) * per_part]

    def leave(number):
        rows = pl.ds(pl.multiple_of(number * part, part), part)
        return pltpu.make_async_copy(out_ref.at[rows], out_hbm.at[rows], left.at[number])

    def finish(number):
        grads = [grads_ref[j * lanes : (j + 1) * lanes, :] for j in range(per_part)]
        sums = [jnp.sum(g * g, axis=1, keepdims=True) for g in grads]
        state = turned[number, :, :per_part] + jnp.concatenate(sums, axis=1) * (1.0 / features)
        turned_new[number, :, :per_part] = state
        scale = learn_rate / (jnp.sqrt(state) + adagrad_eps)
        for j in range(per_part):
            place = pl.ds(pl.multiple_of(number * part + j * lanes, lanes), lanes)
            out_ref[place, :] = table_ref[place, :] - grads[j] * scale[:, j : j + 1]

    def with_blocks(take_blocks):
        rows_held = held[: take_blocks * batch].reshape(take_blocks * batch * wide, features)

        def gather(number):
            row_of = iota((part, wide), 0) + number * part
            picker = jnp.concatenate(
                [
                    (packed[k : k + 1, :] == row_of).astype(f32).astype(bf16)
                    for k in range(take_blocks * batch)
                ],
                axis=1,
            )
            return mul(picker, rows_held)

        def step(number, carry):
            finish(number - 1)
            grads_ref[...] = gather(number)
            leave(number - 1).start()
            return carry

        grads_ref[...] = gather(0)
        lax.fori_loop(1, parts, step, 0)

    first = max(1, total_blocks // 2)
    for take_blocks in range(first, total_blocks + 1):
        chosen = blocks <= first if take_blocks == first else blocks == take_blocks
        pl.when(chosen)(partial(with_blocks, take_blocks))

    finish(parts - 1)
    leave(parts - 1).start()
    for number in range(parts):
        new_state_ref[number * per_part : (number + 1) * per_part, :] = jnp.transpose(
            turned_new[number]
        )[:per_part]
    for number in range(parts):
        leave(number).wait()


def update(asked, returned, table, state):
    peers, stride = asked.shape
    rows_dev, features = table.shape
    wide = pl.cdiv(stride, lanes) * lanes
    part = min(512, rows_dev)
    parts = rows_dev // part
    new_table, new_state = pl.pallas_call(
        update_kernel,
        out_shape=(
            jax.ShapeDtypeStruct(table.shape, f32),
            jax.ShapeDtypeStruct((rows_dev // lanes, lanes), f32),
        ),
        in_specs=[in_vmem, in_vmem, in_vmem, in_vmem],
        out_specs=(in_hbm, in_vmem),
        scratch_shapes=active_scratch(peers, stride)
        + [
            pltpu.VMEM((pl.cdiv(peers, batch) * batch, wide, features), bf16),
            pltpu.VMEM((parts, lanes, lanes), f32),
            pltpu.VMEM((parts, lanes, lanes), f32),
            pltpu.VMEM((part, features), f32),
            pltpu.VMEM(table.shape, f32),
            pltpu.SemaphoreType.DMA((parts,)),
        ],
        compiler_params=params(48),
        name="update",
    )(asked, returned, table, state.reshape(rows_dev // lanes, lanes))
    return new_table, new_state.reshape(rows_dev)


def body(
    embeddings,
    adagrad_state,
    edge_count,
    lhs_owner,
    lhs_row,
    rhs_owner,
    rhs_row,
    neg_owner,
    neg_row,
):
    axes = ("dom", "group")
    rows_dev = embeddings.shape[0]
    group_len = lhs_row.shape[2]
    peers = lax.axis_size("dom") * lax.axis_size("group")
    cap = pl.cdiv(5 * group_len // (4 * peers), 8) * 8
    indices = [
        x.reshape(1, group_len)
        for x in (lhs_owner, lhs_row, rhs_owner, rhs_row, neg_owner, neg_row)
    ]
    ask, spots, fill = prep(edge_count, indices, peers, cap, rows_dev)
    asked = lax.all_to_all(ask, axes, split_axis=0, concat_axis=0, tiled=True)
    answer = fetch(asked, embeddings.astype(bf16))
    arrived = lax.all_to_all(answer, axes, split_axis=0, concat_axis=0, tiled=True)
    grads = train(spots, fill, arrived)
    returned = lax.all_to_all(grads, axes, split_axis=0, concat_axis=0, tiled=True)
    return update(asked, returned, embeddings, adagrad_state)


def solution(mesh):
    return jax.shard_map(
        body,
        mesh=mesh,
        in_specs=(
            P(("dom", "group"), None),
            P(("dom", "group")),
            P("dom"),
            P("dom", "group", None, None),
            P("dom", "group", None),
            P("dom", "group", None, None),
            P("dom", "group", None),
            P("dom", "group", None, None),
            P("dom", "group", None),
        ),
        out_specs=(P(("dom", "group"), None), P(("dom", "group"))),
        check_vma=False,
    )
```

```python
from functools import partial

import jax
import jax.numpy as jnp
from jax import lax
from jax.experimental import pallas as pl
from jax.experimental.pallas import tpu as pltpu
from jax.sharding import PartitionSpec as P

learn_rate = 0.1
adagrad_eps = 1e-06
lanes = 128
in_vmem = pl.BlockSpec(memory_space=pltpu.VMEM)
in_smem = pl.BlockSpec(memory_space=pltpu.SMEM)
in_hbm = pl.BlockSpec(memory_space=pltpu.HBM)
by_rows = (((1,), (1,)), ((), ()))
f32, bf16, i32 = jnp.float32, jnp.bfloat16, jnp.int32


def params(mib):
    return pltpu.CompilerParams(vmem_limit_bytes=mib * 2**20)


def mul(a, b):
    return jnp.dot(a, b, preferred_element_type=f32)


def mul_t(a, b):
    return lax.dot_general(a, b, by_rows, preferred_element_type=f32)


def iota(shape, dim):
    return lax.broadcasted_iota(i32, shape, dim)


def prep_kernel(rows_dev, wide, stride, count_hbm, *refs):
    index_hbm, message_ref = refs[:6], refs[6]
    index_refs, edges, arrivals = refs[7:13], refs[13], refs[14]
    copies = [
        pltpu.make_async_copy(source, target, arrivals.at[number])
        for number, (source, target) in enumerate(
            zip((count_hbm, *index_hbm), (edges, *index_refs))
        )
    ]
    for copy in copies:
        copy.start()
    peers = message_ref.shape[0]
    cap = stride // 3
    count = index_refs[0].shape[1]
    part = min(256, count)
    upper = (iota((part, part), 0) < iota((part, part), 1)).astype(f32).astype(bf16)
    peer_of = iota((peers, count), 0)
    slot_of = iota((wide, count), 0).astype(f32)
    for copy in copies:
        copy.wait()
    limit = jnp.clip(edges[0] - lax.axis_index("group") * count, 0, count)
    limit = jnp.full((1, 1), limit, i32)
    live = (iota((1, count), 1) < limit).astype(f32)
    active = (limit > 0).astype(f32)
    matches, ranks, sizes = [], [], []
    for kind in range(3):
        match = (index_refs[2 * kind][...] == peer_of).astype(f32)
        match = match * (active if kind == 2 else live)
        seen = jnp.zeros((peers, 1), f32)
        pieces = []
        for start in range(0, count, part):
            now = match[:, start : start + part]
            before = mul(now.astype(bf16), upper) + seen
            seen = seen + jnp.sum(now, axis=1, keepdims=True)
            pieces.append(jnp.sum(now * before, axis=0, keepdims=True))
        matches.append(match.astype(bf16))
        ranks.append(jnp.concatenate(pieces, axis=1))
        most = jnp.max(seen, axis=0, keepdims=True).astype(i32)
        sizes.append(((most + 7) // 8 * 8).astype(f32))
    starts = [jnp.zeros((1, 1), f32), sizes[0], sizes[0] + sizes[1]]
    high = low = there = jnp.zeros((peers, wide), f32)
    for kind in range(3):
        row = index_refs[2 * kind + 1][...]
        slot = (ranks[kind] + starts[kind] == slot_of).astype(f32)
        high += mul_t(matches[kind], (slot * (row // 64).astype(f32)).astype(bf16))
        low += mul_t(matches[kind], (slot * (row % 64).astype(f32)).astype(bf16))
        there += mul_t(matches[kind], slot.astype(bf16))
    said = jnp.where(there > 0.5, high * 64.0 + low, float(rows_dev))
    lane = iota((peers, wide), 1) - stride
    for number, value in enumerate((starts[2] + sizes[2], limit.astype(f32), starts[1], starts[2])):
        said = jnp.where(lane == number, value, said)
    said = said.astype(i32)
    shared = mul_t(jnp.ones((8, count), bf16), matches[2])[0:1, :]
    shared = shared.astype(i32)
    spots = [
        jnp.where(live > 0.5, index_refs[2 * kind][...].astype(f32) * cap + ranks[kind], 4095.0)
        for kind in range(2)
    ]
    spots = (spots[0] * 4096.0 + spots[1]).astype(i32)
    for peer in range(peers):
        message_ref[peer, :, :wide] = said[peer : peer + 1]
        message_ref[peer, :, wide : wide + peers] = shared
        message_ref[peer, :, message_ref.shape[2] - count :] = spots


def up_to_lanes(size):
    return pl.cdiv(size, lanes) * lanes


def prep(edge_count, indices, peers, stride, rows_dev):
    count = indices[0].shape[1]
    wide = up_to_lanes(stride + 8)
    return pl.pallas_call(
        partial(prep_kernel, rows_dev, wide, stride),
        out_shape=jax.ShapeDtypeStruct((peers, 1, wide + up_to_lanes(peers) + count), i32),
        in_specs=[pl.BlockSpec(memory_space=pl.ANY)] + [in_hbm] * 6,
        out_specs=in_vmem,
        scratch_shapes=[pltpu.VMEM((1, count), i32)] * 6
        + [pltpu.SMEM((1,), i32), pltpu.SemaphoreType.DMA((7,))],
        compiler_params=params(62),
        name="prep",
    )(edge_count, *indices)


def plan_kernel(sizes, wide, stride, rows_dev, got_ref, choice_ref, info_ref, rows_ref):
    peers = got_ref.shape[0]
    chips = peers // 2
    heads = got_ref[:, :wide]
    down = heads[:, stride : stride + 1].astype(f32)
    across = jnp.transpose(jnp.broadcast_to(down, (peers, lanes)))[0:1, :]
    u, t = iota((peers, peers), 0), iota((peers, peers), 1)
    ahead = (down > across) | ((down == across) & (u < t))
    rank = jnp.sum(ahead.astype(f32), axis=0, keepdims=True)
    chip = jnp.where(rank < chips, rank, peers - 1 - rank)
    held = (iota((chips, peers), 0).astype(f32) == chip).astype(f32) * across
    need = jnp.max(jnp.sum(held, axis=1, keepdims=True))
    choice = jnp.int32(0)
    for size in sizes[:-1]:
        choice = choice + (need > 2.0 * size).astype(i32)
    choice_ref[0] = choice
    alone = choice == len(sizes) - 1
    me = lax.axis_index("dom") * lax.axis_size("group") + lax.axis_index("group")
    mine = (me // 2).astype(f32)
    want = jnp.where(me % 2 == 0, mine, peers - 1 - mine)
    want = jnp.where(alone, me.astype(f32), want)
    place = iota((1, peers), 1).astype(f32)
    group = jnp.sum((rank == want).astype(f32) * place).astype(i32)
    first = jnp.sum((rank == mine).astype(f32) * across, axis=1, keepdims=True).astype(i32)
    size = jnp.int32(sizes[0])
    for number in range(1, len(sizes)):
        size = jnp.where(choice == number, sizes[number], size)
    base = (jnp.maximum(first, size) - size) * (me % 2)
    info = got_ref[pl.ds(group, 1), :]
    info = jnp.where(iota(info.shape, 1) == stride + 4, base, info)
    info_ref[...] = jnp.broadcast_to(info, info_ref.shape)
    asked = jnp.where(iota(heads.shape, 1) < stride, heads, rows_dev)
    high, low = (asked // 64).astype(f32).astype(bf16), (asked % 64).astype(f32).astype(bf16)
    chip_down, device_down = (u // 2).astype(f32), u.astype(f32)
    for number, wanted in enumerate((chip_down, peers - 1 - chip_down)):
        chosen = (rank == jnp.where(alone, device_down, wanted)).astype(f32)
        if number == 0:
            sent = jnp.sum(chosen * across, axis=1, keepdims=True)
            sent = jnp.where(alone, jnp.sum((across > 0.0).astype(f32)), sent)
            rows_ref[2] = jnp.broadcast_to(sent, (peers, wide)).astype(i32)
        chosen = chosen.astype(bf16)
        rows_ref[number] = (mul(chosen, high) * 64.0 + mul(chosen, low)).astype(i32)


def plan(got, sizes, stride, rows_dev):
    peers, length = got.shape
    wide = up_to_lanes(stride + 8)
    return pl.pallas_call(
        partial(plan_kernel, sizes, wide, stride, rows_dev),
        out_shape=(
            jax.ShapeDtypeStruct((1,), i32),
            jax.ShapeDtypeStruct((8, length), i32),
            jax.ShapeDtypeStruct((3, peers, wide), i32),
        ),
        in_specs=[in_vmem],
        out_specs=(in_smem, in_vmem, in_vmem),
        compiler_params=params(32),
        name="plan",
    )(got)


def block_rows(rows_ref, size, stride):
    first, second, first_size = rows_ref[0], rows_ref[1], rows_ref[2]
    lane, device = iota(first.shape, 1), iota(first.shape, 0)
    offset = jnp.maximum(first_size, size) - size
    after = second
    for shift in range(8, stride - size + 1, 8):
        after = jnp.where(offset == shift, pltpu.roll(second, shift, 1), after)
    if size < stride:
        rest = pltpu.roll(first, first.shape[1] - size, 1)
        after = jnp.where(lane < offset, rest, after)
    rows = jnp.where(device % 2 == 0, first, after)
    return jnp.where(lane < size, rows, -1)


def fetch_kernel(size, stride, rows_ref, table_ref, out_ref, packed):
    rows_dev = table_ref.shape[0]
    asked = block_rows(rows_ref, size, stride)
    for number in range(packed.shape[0]):
        packed[number] = asked[number * 8 : number * 8 + 8]
    row_of = iota((8 * size, rows_dev), 1)

    def block(number, carry):
        columns = jnp.transpose(packed[number])
        column = jnp.concatenate([columns[:size, j : j + 1] for j in range(8)], axis=0)
        picker = (column == row_of).astype(f32).astype(bf16)
        place = pl.ds(pl.multiple_of(number * 8 * size, 8 * size), 8 * size)
        out_ref[place, :] = mul(picker, table_ref[...]).astype(bf16)
        return carry

    blocks = packed.shape[0]
    if size == stride:
        blocks = pl.cdiv(active_devices(rows_ref), 8)

        def empty(number, carry):
            place = pl.ds(pl.multiple_of(number * 8 * size, 8 * size), 8 * size)
            out_ref[place, :] = jnp.zeros((8 * size, out_ref.shape[1]), bf16)
            return carry

        lax.fori_loop(blocks, packed.shape[0], empty, 0)
    lax.fori_loop(0, blocks, block, 0)


def active_devices(rows_ref):
    return jnp.max(rows_ref[2, 0:1, 0:1].astype(f32)).astype(i32)


def fetch(rows, table, size, stride):
    peers, wide = rows.shape[1:]
    return pl.pallas_call(
        partial(fetch_kernel, size, stride),
        out_shape=jax.ShapeDtypeStruct((peers * size, table.shape[1]), bf16),
        in_specs=[in_vmem, in_vmem],
        out_specs=in_vmem,
        scratch_shapes=[pltpu.VMEM((peers // 8, 8, wide), i32)],
        compiler_params=params(40),
        name="fetch",
    )(rows, table)


def train_kernel(
    wide, info_ref, come_ref, go_ref, stage, wide_ref, place_ref, left_ref, right_ref, live_ref,
    gl_ref, pg_ref, ps_ref, pr_ref
):
    peers, stride, features = come_ref.shape
    cap = stride // 3
    slots = peers * cap
    count = left_ref.shape[0]
    part = min(256, count)
    starts = range(0, count, part)

    def told(number):
        return info_ref[0:1, stride + number : stride + number + 1]

    base = jnp.sum(told(4).astype(f32)).astype(i32)
    bases = [base]
    for number in (2, 3):
        bases.append(base + jnp.sum(told(number).astype(f32)).astype(i32))
    bases = [pl.multiple_of(value, 8) for value in bases]
    for peer in range(peers):
        stage[peer, :stride, :] = come_ref[peer].astype(f32)
        stage[peer, stride:, :] = jnp.zeros((stage.shape[1] - stride, features), f32)
    for peer in range(peers):
        for kind in range(3):
            wide_ref[kind, peer * cap : peer * cap + cap, :] = stage[
                peer, pl.ds(bases[kind], cap), :
            ]
    packed_spots = info_ref[:, info_ref.shape[1] - count :]
    spot_rows = [(packed_spots // 4096).astype(f32), (packed_spots % 4096).astype(f32)]
    spot_columns = [jnp.transpose(rows) for rows in spot_rows]
    shared_down = jnp.transpose(info_ref[:, wide : wide + lanes].astype(f32))[:peers, 0:1]
    place = (iota((peers, slots), 1) - iota((peers, slots), 0) * cap).astype(f32)
    filled = ((place >= 0.0) & (place < shared_down)).astype(f32)
    fill = jnp.sum(filled, axis=0, keepdims=True)
    limit = told(1).astype(f32)
    live_across = (iota((1, count), 1).astype(f32) < limit).astype(f32)
    live_down = (iota((count, 1), 0).astype(f32) < limit).astype(f32)
    slot_across = iota((part, slots), 1).astype(f32)
    for kind, target in ((0, left_ref), (1, right_ref)):
        held = wide_ref[kind].astype(bf16)
        for start in starts:
            column = spot_columns[kind][start : start + part, 0:1]
            picker = (column == slot_across).astype(f32).astype(bf16)
            rows = mul(picker, held)
            target[start : start + part, :] = rows.astype(bf16)
            if kind == 1:
                rows = rows * live_down[start : start + part]
                live_ref[start : start + part, :] = rows.astype(bf16)
    shared_rows = wide_ref[2].astype(bf16)
    off_diagonal = (iota((part, part), 0) != iota((part, part), 1)).astype(f32)
    for start in starts:
        here = slice(start, start + part)
        left = left_ref[here, :]
        left_wide = left.astype(f32)
        right_wide = right_ref[here, :].astype(f32)
        pos_exp = jnp.exp(jnp.sum(left_wide * right_wide, axis=1, keepdims=True))
        shared_exp = jnp.exp(mul_t(left, shared_rows)) * fill
        total = pos_exp + jnp.sum(shared_exp, axis=1, keepdims=True)
        chunk_exps = []
        for other in starts:
            chunk_exp = jnp.exp(mul_t(left, right_ref[other : other + part, :]))
            if other == start:
                chunk_exp = chunk_exp * off_diagonal
            counted = chunk_exp * live_across[:, other : other + part]
            total = total + jnp.sum(counted, axis=1, keepdims=True)
            chunk_exps.append(chunk_exp)
        live = live_down[here]
        weight = live / total
        pos_grad = live * (pos_exp / total - 1.0)
        ps_ref[here, :] = (shared_exp * weight).astype(bf16)
        for other, chunk_exp in zip(starts, chunk_exps):
            pr_ref[here, other : other + part] = (chunk_exp * weight).astype(bf16)
        pull = mul(ps_ref[here, :], shared_rows) + mul(pr_ref[here, :], live_ref[...])
        gl_ref[here, :] = (pos_grad * right_wide + pull).astype(bf16)
        pg_ref[here, :] = pos_grad * left_wide
    left_turned = jnp.transpose(left_ref[...].astype(f32)).astype(bf16)
    place_ref[2] = jnp.transpose(mul(left_turned, ps_ref[...]))
    grad_right = jnp.transpose(mul(left_turned, pr_ref[...])) * live_down + pg_ref[...]
    right_ref[...] = grad_right.astype(bf16)
    slot_down = iota((part, count), 0).astype(f32)
    for kind, source in ((0, gl_ref), (1, right_ref)):
        for start in range(0, slots, part):
            picker = spot_rows[kind][0:1, :] - float(start) == slot_down
            picker = picker.astype(f32).astype(bf16)
            place_ref[kind, start : start + part, :] = mul(picker, source[...])
    stage[...] = jnp.zeros(stage.shape, f32)
    for kind in range(3):
        for peer in range(peers):
            stage[peer, pl.ds(bases[kind], cap), :] = place_ref[
                kind, peer * cap : peer * cap + cap, :
            ]
    for peer in range(peers):
        go_ref[peer] = stage[peer, :stride, :].astype(bf16)


def train(info, arrived, count, wide):
    peers, stride, features = arrived.shape
    cap = stride // 3
    slots = peers * cap
    return pl.pallas_call(
        partial(train_kernel, wide),
        out_shape=jax.ShapeDtypeStruct(arrived.shape, bf16),
        in_specs=[in_vmem, in_vmem],
        out_specs=in_vmem,
        scratch_shapes=[
            pltpu.VMEM((peers, stride + cap, features), f32),
            pltpu.VMEM((3, slots, features), f32),
            pltpu.VMEM((3, slots, features), f32),
            pltpu.VMEM((count, features), bf16),
            pltpu.VMEM((count, features), bf16),
            pltpu.VMEM((count, features), bf16),
            pltpu.VMEM((count, features), bf16),
            pltpu.VMEM((count, features), f32),
            pltpu.VMEM((count, slots), bf16),
            pltpu.VMEM((count, count), bf16),
        ],
        compiler_params=params(48),
        name="train",
    )(info, arrived)


def update_kernel(
    size, stride, rows_ref, back_ref, table_ref, state_ref, out_hbm, new_state_ref,
    turned, turned_new, grads_ref, out_ref, left
):
    peers, wide = rows_ref.shape[1:]
    rows_dev, features = table_ref.shape
    part = min(512, rows_dev)
    parts = rows_dev // part
    per_part = part // lanes
    asked = block_rows(rows_ref, size, stride) + 64
    length = peers * size
    spread = (iota((wide, length), 0) == iota((wide, length), 1) % size).astype(f32).astype(bf16)
    in_block = iota((peers, length), 1) // size == iota((peers, length), 0)
    flat = [
        jnp.sum(
            jnp.where(in_block, mul(digit.astype(f32).astype(bf16), spread), 0.0),
            axis=0,
            keepdims=True,
        )
        for digit in (asked // 64, asked % 64)
    ]
    flat = (flat[0] * 64.0 + flat[1]).astype(i32) - 64
    state_turned = jnp.transpose(state_ref[...])
    for number in range(parts):
        turned[number, :, :per_part] = state_turned[:, number * per_part : (number + 1) * per_part]

    def leave(number):
        rows = pl.ds(pl.multiple_of(number * part, part), part)
        return pltpu.make_async_copy(out_ref.at[rows], out_hbm.at[rows], left.at[number])

    def finish(number):
        grads = [grads_ref[j * lanes : (j + 1) * lanes, :] for j in range(per_part)]
        sums = [jnp.sum(g * g, axis=1, keepdims=True) for g in grads]
        state = turned[number, :, :per_part] + jnp.concatenate(sums, axis=1) * (1.0 / features)
        turned_new[number, :, :per_part] = state
        scale = learn_rate / (jnp.sqrt(state) + adagrad_eps)
        for j in range(per_part):
            place = pl.ds(pl.multiple_of(number * part + j * lanes, lanes), lanes)
            out_ref[place, :] = table_ref[place, :] - grads[j] * scale[:, j : j + 1]

    def with_length(length):
        def gather(number):
            picker = flat[:, :length] == iota((part, length), 0) + number * part
            return mul(picker.astype(f32).astype(bf16), back_ref[:length, :])

        def step(number, carry):
            finish(number - 1)
            grads_ref[...] = gather(number)
            leave(number - 1).start()
            return carry

        grads_ref[...] = gather(0)
        lax.fori_loop(1, parts, step, 0)

    if size == stride:
        most = peers * 3 // 4
        few = active_devices(rows_ref) <= most
        pl.when(few)(lambda: with_length(up_to_lanes(most * size)))
        pl.when(jnp.logical_not(few))(lambda: with_length(length))
    else:
        with_length(length)
    finish(parts - 1)
    leave(parts - 1).start()
    for number in range(parts):
        new_state_ref[number * per_part : (number + 1) * per_part, :] = jnp.transpose(
            turned_new[number]
        )[:per_part]
    for number in range(parts):
        leave(number).wait()


def update(rows, returned, table, state, size, stride):
    rows_dev, features = table.shape
    part = min(512, rows_dev)
    parts = rows_dev // part
    new_table, new_state = pl.pallas_call(
        partial(update_kernel, size, stride),
        out_shape=(
            jax.ShapeDtypeStruct(table.shape, f32),
            jax.ShapeDtypeStruct((rows_dev // lanes, lanes), f32),
        ),
        in_specs=[in_vmem, in_vmem, in_vmem, in_vmem],
        out_specs=(in_hbm, in_vmem),
        scratch_shapes=[
            pltpu.VMEM((parts, lanes, lanes), f32),
            pltpu.VMEM((parts, lanes, lanes), f32),
            pltpu.VMEM((part, features), f32),
            pltpu.VMEM(table.shape, f32),
            pltpu.SemaphoreType.DMA((parts,)),
        ],
        compiler_params=params(48),
        name="update",
    )(rows, returned, table, state.reshape(rows_dev // lanes, lanes))
    return new_table, new_state.reshape(rows_dev)


def body(
    embeddings,
    adagrad_state,
    edge_count,
    lhs_owner,
    lhs_row,
    rhs_owner,
    rhs_row,
    neg_owner,
    neg_row,
):
    axes = ("dom", "group")
    rows_dev, features = embeddings.shape
    group_len = lhs_row.shape[2]
    group_size = lax.axis_size("group")
    peers = lax.axis_size("dom") * group_size
    stride = 3 * (pl.cdiv(5 * group_len // (4 * peers), 8) * 8)
    half = pl.cdiv(stride // 2, 8) * 8
    sizes = sorted({half, min(half + 16, stride), min(half + 24, stride), stride})
    indices = [
        x.reshape(1, group_len)
        for x in (lhs_owner, lhs_row, rhs_owner, rhs_row, neg_owner, neg_row)
    ]

    def exchange(blocks):
        return lax.all_to_all(blocks, axes, split_axis=0, concat_axis=0, tiled=True)

    def bring(size):
        def run(rows, table16):
            answer = fetch(rows, table16, size, stride).reshape(peers, size, features)
            arrived = exchange(answer)
            if size == stride:
                return arrived
            to_first = [(core, core - 1) for core in range(1, group_size, 2)]
            extra = lax.ppermute(arrived[:, : stride - size], "group", to_first)
            return jnp.concatenate([arrived, extra], axis=1)

        return run

    def take(size):
        def run(rows, grads, table, state):
            over = stride - size
            outgoing = grads
            if over:
                to_second = [(core - 1, core) for core in range(1, group_size, 2)]
                passed = lax.ppermute(grads[:, size:], "group", to_second)
                outgoing = jnp.concatenate(
                    [grads[:, :over] + passed, grads[:, over:size]], axis=1
                )
            returned = exchange(outgoing).reshape(peers * size, features)
            return update(rows, returned, table, state, size, stride)

        return run

    got = exchange(prep(edge_count, indices, peers, stride, rows_dev)).reshape(peers, -1)
    choice, info, rows = plan(got, sizes, stride, rows_dev)
    number = choice[0]
    arrived = lax.switch(
        number, [bring(size) for size in sizes], rows, embeddings.astype(bf16)
    )
    grads = train(info, arrived, group_len, up_to_lanes(stride + 8))
    return lax.switch(
        number, [take(size) for size in sizes], rows, grads, embeddings, adagrad_state
    )


def solution(mesh):
    return jax.shard_map(
        body,
        mesh=mesh,
        in_specs=(
            P(("dom", "group"), None),
            P(("dom", "group")),
            P("dom"),
            P("dom", "group", None, None),
            P("dom", "group", None),
            P("dom", "group", None, None),
            P("dom", "group", None),
            P("dom", "group", None, None),
            P("dom", "group", None),
        ),
        out_specs=(P(("dom", "group"), None), P(("dom", "group"))),
        check_vma=False,
    )
```

```python
from functools import partial

import jax
import jax.numpy as jnp
from jax import lax
from jax.experimental import pallas as pl
from jax.experimental.pallas import tpu as pltpu
from jax.sharding import PartitionSpec as P

learn_rate = 0.1
adagrad_eps = 1e-06
lanes = 128
in_vmem = pl.BlockSpec(memory_space=pltpu.VMEM)
in_smem = pl.BlockSpec(memory_space=pltpu.SMEM)
in_hbm = pl.BlockSpec(memory_space=pltpu.HBM)
by_rows = (((1,), (1,)), ((), ()))
f32, bf16, i32 = jnp.float32, jnp.bfloat16, jnp.int32


def params(mib):
    return pltpu.CompilerParams(vmem_limit_bytes=mib * 2**20)


def mul(a, b):
    return jnp.dot(a, b, preferred_element_type=f32)


def mul_t(a, b):
    return lax.dot_general(a, b, by_rows, preferred_element_type=f32)


def iota(shape, dim):
    return lax.broadcasted_iota(i32, shape, dim)


def prep_kernel(rows_dev, wide, stride, count_hbm, *refs):
    index_hbm, message_ref = refs[:6], refs[6]
    index_refs, edges, arrivals = refs[7:13], refs[13], refs[14]
    copies = [
        pltpu.make_async_copy(source, target, arrivals.at[number])
        for number, (source, target) in enumerate(
            zip((count_hbm, *index_hbm), (edges, *index_refs))
        )
    ]
    for copy in copies:
        copy.start()
    peers = message_ref.shape[0]
    cap = stride // 3
    count = index_refs[0].shape[1]
    part = min(256, count)
    upper = (iota((part, part), 0) < iota((part, part), 1)).astype(f32).astype(bf16)
    peer_of = iota((peers, count), 0)
    slot_of = iota((wide, count), 0).astype(f32)
    for copy in copies:
        copy.wait()
    limit = jnp.clip(edges[0] - lax.axis_index("group") * count, 0, count)
    limit = jnp.full((1, 1), limit, i32)
    live = (iota((1, count), 1) < limit).astype(f32)
    active = (limit > 0).astype(f32)
    matches, ranks, sizes = [], [], []
    for kind in range(3):
        match = (index_refs[2 * kind][...] == peer_of).astype(f32)
        match = match * (active if kind == 2 else live)
        seen = jnp.zeros((peers, 1), f32)
        pieces = []
        for start in range(0, count, part):
            now = match[:, start : start + part]
            before = mul(now.astype(bf16), upper) + seen
            seen = seen + jnp.sum(now, axis=1, keepdims=True)
            pieces.append(jnp.sum(now * before, axis=0, keepdims=True))
        matches.append(match.astype(bf16))
        ranks.append(jnp.concatenate(pieces, axis=1))
        most = jnp.max(seen, axis=0, keepdims=True).astype(i32)
        sizes.append(((most + 7) // 8 * 8).astype(f32))
    starts = [jnp.zeros((1, 1), f32), sizes[0], sizes[0] + sizes[1]]
    high = low = there = jnp.zeros((peers, wide), f32)
    for kind in range(3):
        row = index_refs[2 * kind + 1][...]
        slot = (ranks[kind] + starts[kind] == slot_of).astype(f32)
        high += mul_t(matches[kind], (slot * (row // 64).astype(f32)).astype(bf16))
        low += mul_t(matches[kind], (slot * (row % 64).astype(f32)).astype(bf16))
        there += mul_t(matches[kind], slot.astype(bf16))
    said = jnp.where(there > 0.5, high * 64.0 + low, float(rows_dev))
    lane = iota((peers, wide), 1) - stride
    for number, value in enumerate((starts[2] + sizes[2], limit.astype(f32), starts[1], starts[2])):
        said = jnp.where(lane == number, value, said)
    said = said.astype(i32)
    shared = mul_t(jnp.ones((8, count), bf16), matches[2])[0:1, :]
    shared = shared.astype(i32)
    spots = [
        jnp.where(live > 0.5, index_refs[2 * kind][...].astype(f32) * cap + ranks[kind], 4095.0)
        for kind in range(2)
    ]
    spots = (spots[0] * 4096.0 + spots[1]).astype(i32)
    for peer in range(peers):
        message_ref[peer, :, :wide] = said[peer : peer + 1]
        message_ref[peer, :, wide : wide + peers] = shared
        message_ref[peer, :, message_ref.shape[2] - count :] = spots


def up_to_lanes(size):
    return pl.cdiv(size, lanes) * lanes


def prep(edge_count, indices, peers, stride, rows_dev):
    count = indices[0].shape[1]
    wide = up_to_lanes(stride + 8)
    return pl.pallas_call(
        partial(prep_kernel, rows_dev, wide, stride),
        out_shape=jax.ShapeDtypeStruct((peers, 1, wide + up_to_lanes(peers) + count), i32),
        in_specs=[pl.BlockSpec(memory_space=pl.ANY)] + [in_hbm] * 6,
        out_specs=in_vmem,
        scratch_shapes=[pltpu.VMEM((1, count), i32)] * 6
        + [pltpu.SMEM((1,), i32), pltpu.SemaphoreType.DMA((7,))],
        compiler_params=params(62),
        name="prep",
    )(edge_count, *indices)


def plan_kernel(sizes, wide, stride, rows_dev, got_ref, choice_ref, info_ref, rows_ref):
    peers = got_ref.shape[0]
    chips = peers // 2
    heads = got_ref[:, :wide]
    down = heads[:, stride : stride + 1].astype(f32)
    across = jnp.transpose(jnp.broadcast_to(down, (peers, lanes)))[0:1, :]
    u, t = iota((peers, peers), 0), iota((peers, peers), 1)
    ahead = (down > across) | ((down == across) & (u < t))
    rank = jnp.sum(ahead.astype(f32), axis=0, keepdims=True)
    chip = jnp.where(rank < chips, rank, peers - 1 - rank)
    held = (iota((chips, peers), 0).astype(f32) == chip).astype(f32) * across
    need = jnp.max(jnp.sum(held, axis=1, keepdims=True))
    choice = jnp.int32(0)
    for size in sizes[:-1]:
        choice = choice + (need > 2.0 * size).astype(i32)
    choice_ref[0] = choice
    alone = choice == len(sizes) - 1
    me = lax.axis_index("dom") * lax.axis_size("group") + lax.axis_index("group")
    mine = (me // 2).astype(f32)
    want = jnp.where(me % 2 == 0, mine, peers - 1 - mine)
    want = jnp.where(alone, me.astype(f32), want)
    place = iota((1, peers), 1).astype(f32)
    group = jnp.sum((rank == want).astype(f32) * place).astype(i32)
    first = jnp.sum((rank == mine).astype(f32) * across, axis=1, keepdims=True).astype(i32)
    size = jnp.int32(sizes[0])
    for number in range(1, len(sizes)):
        size = jnp.where(choice == number, sizes[number], size)
    base = (jnp.maximum(first, size) - size) * (me % 2)
    info = got_ref[pl.ds(group, 1), :]
    info = jnp.where(iota(info.shape, 1) == stride + 4, base, info)
    info_ref[...] = jnp.broadcast_to(info, info_ref.shape)
    asked = jnp.where(iota(heads.shape, 1) < stride, heads, rows_dev)
    high, low = (asked // 64).astype(f32).astype(bf16), (asked % 64).astype(f32).astype(bf16)
    chip_down, device_down = (u // 2).astype(f32), u.astype(f32)
    for number, wanted in enumerate((chip_down, peers - 1 - chip_down)):
        chosen = (rank == jnp.where(alone, device_down, wanted)).astype(f32)
        if number == 0:
            sent = jnp.sum(chosen * across, axis=1, keepdims=True)
            sent = jnp.where(alone, jnp.sum((across > 0.0).astype(f32)), sent)
            rows_ref[2] = jnp.broadcast_to(sent, (peers, wide)).astype(i32)
        chosen = chosen.astype(bf16)
        rows_ref[number] = (mul(chosen, high) * 64.0 + mul(chosen, low)).astype(i32)


def plan(got, sizes, stride, rows_dev):
    peers, length = got.shape
    wide = up_to_lanes(stride + 8)
    return pl.pallas_call(
        partial(plan_kernel, sizes, wide, stride, rows_dev),
        out_shape=(
            jax.ShapeDtypeStruct((1,), i32),
            jax.ShapeDtypeStruct((8, length), i32),
            jax.ShapeDtypeStruct((3, peers, wide), i32),
        ),
        in_specs=[in_vmem],
        out_specs=(in_smem, in_vmem, in_vmem),
        compiler_params=params(32),
        name="plan",
    )(got)


def block_rows(rows_ref, size, stride):
    first, second, first_size = rows_ref[0], rows_ref[1], rows_ref[2]
    lane, device = iota(first.shape, 1), iota(first.shape, 0)
    offset = jnp.maximum(first_size, size) - size
    after = second
    for shift in range(8, stride - size + 1, 8):
        after = jnp.where(offset == shift, pltpu.roll(second, shift, 1), after)
    if size < stride:
        rest = pltpu.roll(first, first.shape[1] - size, 1)
        after = jnp.where(lane < offset, rest, after)
    rows = jnp.where(device % 2 == 0, first, after)
    return jnp.where(lane < size, rows, -1)


def fetch_kernel(size, stride, rows_ref, table_ref, out_ref, packed):
    rows_dev = table_ref.shape[0]
    asked = block_rows(rows_ref, size, stride)
    for number in range(packed.shape[0]):
        packed[number] = asked[number * 8 : number * 8 + 8]
    row_of = iota((8 * size, rows_dev), 1)

    def block(number, carry):
        columns = jnp.transpose(packed[number])
        column = jnp.concatenate([columns[:size, j : j + 1] for j in range(8)], axis=0)
        picker = (column == row_of).astype(f32).astype(bf16)
        place = pl.ds(pl.multiple_of(number * 8 * size, 8 * size), 8 * size)
        out_ref[place, :] = mul(picker, table_ref[...]).astype(bf16)
        return carry

    blocks = packed.shape[0]
    if size == stride:
        blocks = pl.cdiv(active_devices(rows_ref), 8)

        def empty(number, carry):
            place = pl.ds(pl.multiple_of(number * 8 * size, 8 * size), 8 * size)
            out_ref[place, :] = jnp.zeros((8 * size, out_ref.shape[1]), bf16)
            return carry

        lax.fori_loop(blocks, packed.shape[0], empty, 0)
    lax.fori_loop(0, blocks, block, 0)


def active_devices(rows_ref):
    return jnp.max(rows_ref[2, 0:1, 0:1].astype(f32)).astype(i32)


def fetch(rows, table, size, stride):
    peers, wide = rows.shape[1:]
    return pl.pallas_call(
        partial(fetch_kernel, size, stride),
        out_shape=jax.ShapeDtypeStruct((peers * size, table.shape[1]), bf16),
        in_specs=[in_vmem, in_vmem],
        out_specs=in_vmem,
        scratch_shapes=[pltpu.VMEM((peers // 8, 8, wide), i32)],
        compiler_params=params(40),
        name="fetch",
    )(rows, table)


def train_kernel(
    wide, info_ref, come_ref, go_ref, stage, wide_ref, place_ref, left_ref, right_ref, live_ref,
    gl_ref, pg_ref, ps_ref, pr_ref
):
    peers, stride, features = come_ref.shape
    cap = stride // 3
    slots = peers * cap
    count = left_ref.shape[0]
    part = min(256, count)
    starts = range(0, count, part)

    def told(number):
        return info_ref[0:1, stride + number : stride + number + 1]

    base = jnp.sum(told(4).astype(f32)).astype(i32)
    bases = [base]
    for number in (2, 3):
        bases.append(base + jnp.sum(told(number).astype(f32)).astype(i32))
    bases = [pl.multiple_of(value, 8) for value in bases]
    for peer in range(peers):
        stage[peer, :stride, :] = come_ref[peer].astype(f32)
        stage[peer, stride:, :] = jnp.zeros((stage.shape[1] - stride, features), f32)
    for peer in range(peers):
        for kind in range(3):
            wide_ref[kind, peer * cap : peer * cap + cap, :] = stage[
                peer, pl.ds(bases[kind], cap), :
            ]
    packed_spots = info_ref[:, info_ref.shape[1] - count :]
    spot_rows = [(packed_spots // 4096).astype(f32), (packed_spots % 4096).astype(f32)]
    spot_columns = [jnp.transpose(rows) for rows in spot_rows]
    shared_down = jnp.transpose(info_ref[:, wide : wide + lanes].astype(f32))[:peers, 0:1]
    place = (iota((peers, slots), 1) - iota((peers, slots), 0) * cap).astype(f32)
    filled = ((place >= 0.0) & (place < shared_down)).astype(f32)
    fill = jnp.sum(filled, axis=0, keepdims=True)
    limit = told(1).astype(f32)
    live_across = (iota((1, count), 1).astype(f32) < limit).astype(f32)
    live_down = (iota((count, 1), 0).astype(f32) < limit).astype(f32)
    slot_across = iota((part, slots), 1).astype(f32)
    for kind, target in ((0, left_ref), (1, right_ref)):
        held = wide_ref[kind].astype(bf16)
        for start in starts:
            column = spot_columns[kind][start : start + part, 0:1]
            picker = (column == slot_across).astype(f32).astype(bf16)
            rows = mul(picker, held)
            target[start : start + part, :] = rows.astype(bf16)
            if kind == 1:
                rows = rows * live_down[start : start + part]
                live_ref[start : start + part, :] = rows.astype(bf16)
    shared_rows = wide_ref[2].astype(bf16)
    off_diagonal = (iota((part, part), 0) != iota((part, part), 1)).astype(f32)
    for start in starts:
        here = slice(start, start + part)
        left = left_ref[here, :]
        left_wide = left.astype(f32)
        right_wide = right_ref[here, :].astype(f32)
        pos_exp = jnp.exp(jnp.sum(left_wide * right_wide, axis=1, keepdims=True))
        shared_exp = jnp.exp(mul_t(left, shared_rows)) * fill
        total = pos_exp + jnp.sum(shared_exp, axis=1, keepdims=True)
        chunk_exps = []
        for other in starts:
            chunk_exp = jnp.exp(mul_t(left, right_ref[other : other + part, :]))
            if other == start:
                chunk_exp = chunk_exp * off_diagonal
            counted = chunk_exp * live_across[:, other : other + part]
            total = total + jnp.sum(counted, axis=1, keepdims=True)
            chunk_exps.append(chunk_exp)
        live = live_down[here]
        weight = live / total
        pos_grad = live * (pos_exp / total - 1.0)
        ps_ref[here, :] = (shared_exp * weight).astype(bf16)
        for other, chunk_exp in zip(starts, chunk_exps):
            pr_ref[here, other : other + part] = (chunk_exp * weight).astype(bf16)
        pull = mul(ps_ref[here, :], shared_rows) + mul(pr_ref[here, :], live_ref[...])
        gl_ref[here, :] = (pos_grad * right_wide + pull).astype(bf16)
        pg_ref[here, :] = pos_grad * left_wide
    left_turned = jnp.transpose(left_ref[...].astype(f32)).astype(bf16)
    place_ref[2] = jnp.transpose(mul(left_turned, ps_ref[...]))
    grad_right = jnp.transpose(mul(left_turned, pr_ref[...])) * live_down + pg_ref[...]
    right_ref[...] = grad_right.astype(bf16)
    slot_down = iota((part, count), 0).astype(f32)
    for kind, source in ((0, gl_ref), (1, right_ref)):
        for start in range(0, slots, part):
            picker = spot_rows[kind][0:1, :] - float(start) == slot_down
            picker = picker.astype(f32).astype(bf16)
            place_ref[kind, start : start + part, :] = mul(picker, source[...])
    stage[:, :stride, :] = jnp.zeros((peers, stride, features), f32)
    for kind in range(3):
        for peer in range(peers):
            stage[peer, pl.ds(bases[kind], cap), :] = place_ref[
                kind, peer * cap : peer * cap + cap, :
            ]
    for peer in range(peers):
        go_ref[peer] = stage[peer, :stride, :].astype(bf16)


def train(info, arrived, count, wide):
    peers, stride, features = arrived.shape
    cap = stride // 3
    slots = peers * cap
    return pl.pallas_call(
        partial(train_kernel, wide),
        out_shape=jax.ShapeDtypeStruct(arrived.shape, bf16),
        in_specs=[in_vmem, in_vmem],
        out_specs=in_vmem,
        scratch_shapes=[
            pltpu.VMEM((peers, stride + cap, features), f32),
            pltpu.VMEM((3, slots, features), f32),
            pltpu.VMEM((3, slots, features), f32),
            pltpu.VMEM((count, features), bf16),
            pltpu.VMEM((count, features), bf16),
            pltpu.VMEM((count, features), bf16),
            pltpu.VMEM((count, features), bf16),
            pltpu.VMEM((count, features), f32),
            pltpu.VMEM((count, slots), bf16),
            pltpu.VMEM((count, count), bf16),
        ],
        compiler_params=params(48),
        name="train",
    )(info, arrived)


def update_kernel(
    size, stride, rows_ref, back_ref, table_ref, state_ref, out_hbm, new_state_ref,
    turned, turned_new, grads_ref, out_ref, came, left
):
    peers, wide = rows_ref.shape[1:]
    rows_dev, features = table_ref.shape
    staged = size == stride
    part = min(512, rows_dev)
    parts = rows_dev // part
    per_part = part // lanes

    def come(number):
        rows = pl.ds(pl.multiple_of(number * part, part), part)
        return pltpu.make_async_copy(table_ref.at[rows], out_ref.at[rows], came.at[number])

    if staged:
        for number in range(parts):
            come(number).start()
    asked = block_rows(rows_ref, size, stride) + 64
    length = peers * size
    spread = (iota((wide, length), 0) == iota((wide, length), 1) % size).astype(f32).astype(bf16)
    in_block = iota((peers, length), 1) // size == iota((peers, length), 0)
    flat = [
        jnp.sum(
            jnp.where(in_block, mul(digit.astype(f32).astype(bf16), spread), 0.0),
            axis=0,
            keepdims=True,
        )
        for digit in (asked // 64, asked % 64)
    ]
    flat = (flat[0] * 64.0 + flat[1]).astype(i32) - 64
    state_turned = jnp.transpose(state_ref[...])
    for number in range(parts):
        turned[number, :, :per_part] = state_turned[:, number * per_part : (number + 1) * per_part]

    def leave(number):
        rows = pl.ds(pl.multiple_of(number * part, part), part)
        return pltpu.make_async_copy(out_ref.at[rows], out_hbm.at[rows], left.at[number])

    def finish(number):
        if staged:
            come(number).wait()
        old_ref = out_ref if staged else table_ref
        grads = [grads_ref[j * lanes : (j + 1) * lanes, :] for j in range(per_part)]
        sums = [jnp.sum(g * g, axis=1, keepdims=True) for g in grads]
        state = turned[number, :, :per_part] + jnp.concatenate(sums, axis=1) * (1.0 / features)
        turned_new[number, :, :per_part] = state
        scale = learn_rate / (jnp.sqrt(state) + adagrad_eps)
        for j in range(per_part):
            place = pl.ds(pl.multiple_of(number * part + j * lanes, lanes), lanes)
            out_ref[place, :] = old_ref[place, :] - grads[j] * scale[:, j : j + 1]

    def with_length(length):
        def gather(number):
            picker = flat[:, :length] == iota((part, length), 0) + number * part
            return mul(picker.astype(f32).astype(bf16), back_ref[:length, :])

        def step(number, carry):
            finish(number - 1)
            grads_ref[...] = gather(number)
            leave(number - 1).start()
            return carry

        grads_ref[...] = gather(0)
        lax.fori_loop(1, parts, step, 0)

    if size == stride:
        most = peers * 3 // 4
        few = active_devices(rows_ref) <= most
        pl.when(few)(lambda: with_length(up_to_lanes(most * size)))
        pl.when(jnp.logical_not(few))(lambda: with_length(length))
    else:
        with_length(length)
    finish(parts - 1)
    leave(parts - 1).start()
    for number in range(parts):
        new_state_ref[number * per_part : (number + 1) * per_part, :] = jnp.transpose(
            turned_new[number]
        )[:per_part]
    for number in range(parts):
        leave(number).wait()


def update(rows, returned, table, state, size, stride):
    rows_dev, features = table.shape
    part = min(512, rows_dev)
    parts = rows_dev // part
    new_table, new_state = pl.pallas_call(
        partial(update_kernel, size, stride),
        out_shape=(
            jax.ShapeDtypeStruct(table.shape, f32),
            jax.ShapeDtypeStruct((rows_dev // lanes, lanes), f32),
        ),
        in_specs=[in_vmem, in_vmem, in_hbm if size == stride else in_vmem, in_vmem],
        out_specs=(in_hbm, in_vmem),
        scratch_shapes=[
            pltpu.VMEM((parts, lanes, lanes), f32),
            pltpu.VMEM((parts, lanes, lanes), f32),
            pltpu.VMEM((part, features), f32),
            pltpu.VMEM(table.shape, f32),
            pltpu.SemaphoreType.DMA((parts,)),
            pltpu.SemaphoreType.DMA((parts,)),
        ],
        compiler_params=params(48),
        name="update",
    )(rows, returned, table, state.reshape(rows_dev // lanes, lanes))
    return new_table, new_state.reshape(rows_dev)


def body(
    embeddings,
    adagrad_state,
    edge_count,
    lhs_owner,
    lhs_row,
    rhs_owner,
    rhs_row,
    neg_owner,
    neg_row,
):
    axes = ("dom", "group")
    rows_dev, features = embeddings.shape
    group_len = lhs_row.shape[2]
    group_size = lax.axis_size("group")
    peers = lax.axis_size("dom") * group_size
    stride = 3 * (pl.cdiv(5 * group_len // (4 * peers), 8) * 8)
    half = pl.cdiv(stride // 2, 8) * 8
    sizes = sorted({half, min(half + 16, stride), min(half + 24, stride), stride})
    indices = [
        x.reshape(1, group_len)
        for x in (lhs_owner, lhs_row, rhs_owner, rhs_row, neg_owner, neg_row)
    ]

    def exchange(blocks):
        return lax.all_to_all(blocks, axes, split_axis=0, concat_axis=0, tiled=True)

    def bring(size):
        def run(rows, table16):
            answer = fetch(rows, table16, size, stride).reshape(peers, size, features)
            arrived = exchange(answer)
            if size == stride:
                return arrived
            to_first = [(core, core - 1) for core in range(1, group_size, 2)]
            extra = lax.ppermute(arrived[:, : stride - size], "group", to_first)
            return jnp.concatenate([arrived, extra], axis=1)

        return run

    def take(size):
        def run(rows, grads, table, state):
            over = stride - size
            outgoing = grads
            if over:
                to_second = [(core - 1, core) for core in range(1, group_size, 2)]
                passed = lax.ppermute(grads[:, size:], "group", to_second)
                outgoing = jnp.concatenate(
                    [grads[:, :over] + passed, grads[:, over:size]], axis=1
                )
            returned = exchange(outgoing).reshape(peers * size, features)
            return update(rows, returned, table, state, size, stride)

        return run

    got = exchange(prep(edge_count, indices, peers, stride, rows_dev)).reshape(peers, -1)
    choice, info, rows = plan(got, sizes, stride, rows_dev)
    number = choice[0]
    arrived = lax.switch(
        number, [bring(size) for size in sizes], rows, embeddings.astype(bf16)
    )
    grads = train(info, arrived, group_len, up_to_lanes(stride + 8))
    return lax.switch(
        number, [take(size) for size in sizes], rows, grads, embeddings, adagrad_state
    )


def solution(mesh):
    return jax.shard_map(
        body,
        mesh=mesh,
        in_specs=(
            P(("dom", "group"), None),
            P(("dom", "group")),
            P("dom"),
            P("dom", "group", None, None),
            P("dom", "group", None),
            P("dom", "group", None, None),
            P("dom", "group", None),
            P("dom", "group", None, None),
            P("dom", "group", None),
        ),
        out_specs=(P(("dom", "group"), None), P(("dom", "group"))),
        check_vma=False,
    )
```

```python
from functools import partial

import jax
import jax.numpy as jnp
from jax import lax
from jax.experimental import pallas as pl
from jax.experimental.pallas import tpu as pltpu
from jax.sharding import PartitionSpec as P

learn_rate = 0.1
adagrad_eps = 1e-06
lanes = 128
in_vmem = pl.BlockSpec(memory_space=pltpu.VMEM)
in_smem = pl.BlockSpec(memory_space=pltpu.SMEM)
in_hbm = pl.BlockSpec(memory_space=pltpu.HBM)
by_rows = (((1,), (1,)), ((), ()))
f32, bf16, i32 = jnp.float32, jnp.bfloat16, jnp.int32


def params(mib):
    return pltpu.CompilerParams(vmem_limit_bytes=mib * 2**20)


def mul(a, b):
    return jnp.dot(a, b, preferred_element_type=f32)


def mul_t(a, b):
    return lax.dot_general(a, b, by_rows, preferred_element_type=f32)


def iota(shape, dim):
    return lax.broadcasted_iota(i32, shape, dim)


def prep_kernel(rows_dev, wide, stride, count_hbm, *refs):
    index_hbm, message_ref = refs[:6], refs[6]
    index_refs, edges, arrivals = refs[7:13], refs[13], refs[14]
    copies = [
        pltpu.make_async_copy(source, target, arrivals.at[number])
        for number, (source, target) in enumerate(
            zip((count_hbm, *index_hbm), (edges, *index_refs))
        )
    ]
    for copy in copies:
        copy.start()
    peers = message_ref.shape[0]
    cap = stride // 3
    count = index_refs[0].shape[1]
    part = min(256, count)
    upper = (iota((part, part), 0) < iota((part, part), 1)).astype(f32).astype(bf16)
    peer_of = iota((peers, count), 0)
    slot_of = iota((wide, count), 0).astype(f32)
    for copy in copies:
        copy.wait()
    limit = jnp.clip(edges[0] - lax.axis_index("group") * count, 0, count)
    limit = jnp.full((1, 1), limit, i32)
    live = (iota((1, count), 1) < limit).astype(f32)
    active = (limit > 0).astype(f32)
    match = jnp.concatenate(
        [
            (index_refs[2 * kind][...] == peer_of).astype(f32) * (active if kind == 2 else live)
            for kind in range(3)
        ],
        axis=0,
    )
    seen = jnp.zeros((3 * peers, 1), f32)
    pieces = [[], [], []]
    for start in range(0, count, part):
        now = match[:, start : start + part]
        before = now * (mul(now.astype(bf16), upper) + seen)
        seen = seen + jnp.sum(now, axis=1, keepdims=True)
        for kind in range(3):
            mine = before[kind * peers : kind * peers + peers]
            pieces[kind].append(jnp.sum(mine, axis=0, keepdims=True))
    ranks = [jnp.concatenate(piece, axis=1) for piece in pieces]
    match = match.astype(bf16)
    matches = [match[kind * peers : kind * peers + peers] for kind in range(3)]
    sizes = []
    for kind in range(3):
        most = jnp.max(seen[kind * peers : kind * peers + peers], axis=0, keepdims=True)
        sizes.append(((most.astype(i32) + 7) // 8 * 8).astype(f32))
    starts = [jnp.zeros((1, 1), f32), sizes[0], sizes[0] + sizes[1]]
    found = jnp.zeros((peers, 3 * wide), f32)
    for kind in range(3):
        row = index_refs[2 * kind + 1][...]
        slot = (ranks[kind] + starts[kind] == slot_of).astype(f32)
        digits = [slot * (row // 64).astype(f32), slot * (row % 64).astype(f32), slot]
        found += mul_t(matches[kind], jnp.concatenate(digits, axis=0).astype(bf16))
    high, low, there = [found[:, k * wide : k * wide + wide] for k in range(3)]
    said = jnp.where(there > 0.5, high * 64.0 + low, float(rows_dev))
    lane = iota((peers, wide), 1) - stride
    for number, value in enumerate((starts[2] + sizes[2], limit.astype(f32), starts[1], starts[2])):
        said = jnp.where(lane == number, value, said)
    said = said.astype(i32)
    shared = mul_t(jnp.ones((8, count), bf16), matches[2])[0:1, :]
    shared = shared.astype(i32)
    spots = [
        jnp.where(live > 0.5, index_refs[2 * kind][...].astype(f32) * cap + ranks[kind], 4095.0)
        for kind in range(2)
    ]
    spots = (spots[0] * 4096.0 + spots[1]).astype(i32)
    for peer in range(peers):
        message_ref[peer, :, :wide] = said[peer : peer + 1]
        message_ref[peer, :, wide : wide + peers] = shared
        message_ref[peer, :, message_ref.shape[2] - count :] = spots


def up_to_lanes(size):
    return pl.cdiv(size, lanes) * lanes


def prep(edge_count, indices, peers, stride, rows_dev):
    count = indices[0].shape[1]
    wide = up_to_lanes(stride + 8)
    return pl.pallas_call(
        partial(prep_kernel, rows_dev, wide, stride),
        out_shape=jax.ShapeDtypeStruct((peers, 1, wide + up_to_lanes(peers) + count), i32),
        in_specs=[pl.BlockSpec(memory_space=pl.ANY)] + [in_hbm] * 6,
        out_specs=in_vmem,
        scratch_shapes=[pltpu.VMEM((1, count), i32)] * 6
        + [pltpu.SMEM((1,), i32), pltpu.SemaphoreType.DMA((7,))],
        compiler_params=params(62),
        name="prep",
    )(edge_count, *indices)


def plan_kernel(sizes, wide, stride, rows_dev, got_ref, choice_ref, info_ref, rows_ref):
    peers = got_ref.shape[0]
    chips = peers // 2
    heads = got_ref[:, :wide]
    down = heads[:, stride : stride + 1].astype(f32)
    across = jnp.transpose(jnp.broadcast_to(down, (peers, lanes)))[0:1, :]
    u, t = iota((peers, peers), 0), iota((peers, peers), 1)
    ahead = (down > across) | ((down == across) & (u < t))
    rank = jnp.sum(ahead.astype(f32), axis=0, keepdims=True)
    chip = jnp.where(rank < chips, rank, peers - 1 - rank)
    held = (iota((chips, peers), 0).astype(f32) == chip).astype(f32) * across
    need = jnp.max(jnp.sum(held, axis=1, keepdims=True))
    choice = jnp.int32(0)
    for size in sizes[:-1]:
        choice = choice + (need > 2.0 * size).astype(i32)
    choice_ref[0] = choice
    alone = choice == len(sizes) - 1
    me = lax.axis_index("dom") * lax.axis_size("group") + lax.axis_index("group")
    mine = (me // 2).astype(f32)
    want = jnp.where(me % 2 == 0, mine, peers - 1 - mine)
    want = jnp.where(alone, me.astype(f32), want)
    place = iota((1, peers), 1).astype(f32)
    group = jnp.sum((rank == want).astype(f32) * place).astype(i32)
    first = jnp.sum((rank == mine).astype(f32) * across, axis=1, keepdims=True).astype(i32)
    size = jnp.int32(sizes[0])
    for number in range(1, len(sizes)):
        size = jnp.where(choice == number, sizes[number], size)
    base = (jnp.maximum(first, size) - size) * (me % 2)
    info = got_ref[pl.ds(group, 1), :]
    info = jnp.where(iota(info.shape, 1) == stride + 4, base, info)
    info_ref[...] = jnp.broadcast_to(info, info_ref.shape)
    asked = jnp.where(iota(heads.shape, 1) < stride, heads, rows_dev)
    high, low = (asked // 64).astype(f32).astype(bf16), (asked % 64).astype(f32).astype(bf16)
    chip_down, device_down = (u // 2).astype(f32), u.astype(f32)
    for number, wanted in enumerate((chip_down, peers - 1 - chip_down)):
        chosen = (rank == jnp.where(alone, device_down, wanted)).astype(f32)
        if number == 0:
            sent = jnp.sum(chosen * across, axis=1, keepdims=True)
            sent = jnp.where(alone, jnp.sum((across > 0.0).astype(f32)), sent)
            rows_ref[2] = jnp.broadcast_to(sent, (peers, wide)).astype(i32)
        chosen = chosen.astype(bf16)
        rows_ref[number] = (mul(chosen, high) * 64.0 + mul(chosen, low)).astype(i32)


def plan(got, sizes, stride, rows_dev):
    peers, length = got.shape
    wide = up_to_lanes(stride + 8)
    return pl.pallas_call(
        partial(plan_kernel, sizes, wide, stride, rows_dev),
        out_shape=(
            jax.ShapeDtypeStruct((1,), i32),
            jax.ShapeDtypeStruct((8, length), i32),
            jax.ShapeDtypeStruct((3, peers, wide), i32),
        ),
        in_specs=[in_vmem],
        out_specs=(in_smem, in_vmem, in_vmem),
        compiler_params=params(32),
        name="plan",
    )(got)


def block_rows(rows_ref, size, stride):
    first, second, first_size = rows_ref[0], rows_ref[1], rows_ref[2]
    lane, device = iota(first.shape, 1), iota(first.shape, 0)
    offset = jnp.maximum(first_size, size) - size
    after = second
    for shift in range(8, stride - size + 1, 8):
        after = jnp.where(offset == shift, pltpu.roll(second, shift, 1), after)
    if size < stride:
        rest = pltpu.roll(first, first.shape[1] - size, 1)
        after = jnp.where(lane < offset, rest, after)
    rows = jnp.where(device % 2 == 0, first, after)
    return jnp.where(lane < size, rows, -1)


def fetch_kernel(size, stride, rows_ref, table_ref, out_ref, packed):
    rows_dev = table_ref.shape[0]
    asked = block_rows(rows_ref, size, stride)
    for number in range(packed.shape[0]):
        packed[number] = asked[number * 8 : number * 8 + 8]
    row_of = iota((8 * size, rows_dev), 1)

    def block(number, carry):
        columns = jnp.transpose(packed[number])
        column = jnp.concatenate([columns[:size, j : j + 1] for j in range(8)], axis=0)
        picker = (column == row_of).astype(f32).astype(bf16)
        place = pl.ds(pl.multiple_of(number * 8 * size, 8 * size), 8 * size)
        out_ref[place, :] = mul(picker, table_ref[...]).astype(bf16)
        return carry

    blocks = packed.shape[0]
    if size == stride:
        blocks = pl.cdiv(active_devices(rows_ref), 8)

        def empty(number, carry):
            place = pl.ds(pl.multiple_of(number * 8 * size, 8 * size), 8 * size)
            out_ref[place, :] = jnp.zeros((8 * size, out_ref.shape[1]), bf16)
            return carry

        lax.fori_loop(blocks, packed.shape[0], empty, 0)
    lax.fori_loop(0, blocks, block, 0)


def active_devices(rows_ref):
    return jnp.max(rows_ref[2, 0:1, 0:1].astype(f32)).astype(i32)


def fetch(rows, table, size, stride):
    peers, wide = rows.shape[1:]
    return pl.pallas_call(
        partial(fetch_kernel, size, stride),
        out_shape=jax.ShapeDtypeStruct((peers * size, table.shape[1]), bf16),
        in_specs=[in_vmem, in_vmem],
        out_specs=in_vmem,
        scratch_shapes=[pltpu.VMEM((peers // 8, 8, wide), i32)],
        compiler_params=params(40),
        name="fetch",
    )(rows, table)


def train_kernel(
    wide, info_ref, come_ref, go_ref, stage, leave_ref, wide_ref, place_ref, left_ref, right_ref, live_ref,
    gl_ref, pg_ref, ps_ref, pr_ref
):
    peers, stride, features = come_ref.shape
    cap = stride // 3
    slots = peers * cap
    count = left_ref.shape[0]
    part = min(256, count)
    starts = range(0, count, part)

    def told(number):
        return info_ref[0:1, stride + number : stride + number + 1]

    base = jnp.sum(told(4).astype(f32)).astype(i32)
    bases = [base]
    for number in (2, 3):
        bases.append(base + jnp.sum(told(number).astype(f32)).astype(i32))
    bases = [pl.multiple_of(value, 8) for value in bases]
    for peer in range(peers):
        stage[peer, :stride, :] = come_ref[peer].astype(f32)
        stage[peer, stride:, :] = jnp.zeros((stage.shape[1] - stride, features), f32)

    def lay(kind):
        for peer in range(peers):
            wide_ref[kind, peer * cap : peer * cap + cap, :] = stage[
                peer, pl.ds(bases[kind], cap), :
            ]

    lay(0)
    packed_spots = info_ref[:, info_ref.shape[1] - count :]
    spot_rows = [(packed_spots // 4096).astype(f32), (packed_spots % 4096).astype(f32)]
    spot_columns = [jnp.transpose(rows) for rows in spot_rows]
    shared_down = jnp.transpose(info_ref[:, wide : wide + lanes].astype(f32))[:peers, 0:1]
    place = (iota((peers, slots), 1) - iota((peers, slots), 0) * cap).astype(f32)
    filled = ((place >= 0.0) & (place < shared_down)).astype(f32)
    fill = jnp.sum(filled, axis=0, keepdims=True)
    limit = told(1).astype(f32)
    live_across = (iota((1, count), 1).astype(f32) < limit).astype(f32)
    live_down = (iota((count, 1), 0).astype(f32) < limit).astype(f32)
    slot_across = iota((part, slots), 1).astype(f32)
    for kind, target in ((0, left_ref), (1, right_ref)):
        held = wide_ref[kind].astype(bf16)
        lay(kind + 1)
        half = peers // 2
        cleared = leave_ref.at[kind * half : kind * half + half, :stride, :]
        cleared[...] = jnp.zeros((half, stride, features), f32)
        for start in starts:
            column = spot_columns[kind][start : start + part, 0:1]
            picker = (column == slot_across).astype(f32).astype(bf16)
            rows = mul(picker, held)
            target[start : start + part, :] = rows.astype(bf16)
            if kind == 1:
                rows = rows * live_down[start : start + part]
                live_ref[start : start + part, :] = rows.astype(bf16)
    shared_rows = wide_ref[2].astype(bf16)
    off_diagonal = (iota((part, part), 0) != iota((part, part), 1)).astype(f32)
    for start in starts:
        here = slice(start, start + part)
        left = left_ref[here, :]
        left_wide = left.astype(f32)
        right_wide = right_ref[here, :].astype(f32)
        pos_exp = jnp.exp(jnp.sum(left_wide * right_wide, axis=1, keepdims=True))
        shared_exp = jnp.exp(mul_t(left, shared_rows)) * fill
        total = pos_exp + jnp.sum(shared_exp, axis=1, keepdims=True)
        chunk_exps = []
        for other in starts:
            chunk_exp = jnp.exp(mul_t(left, right_ref[other : other + part, :]))
            if other == start:
                chunk_exp = chunk_exp * off_diagonal
            counted = chunk_exp * live_across[:, other : other + part]
            total = total + jnp.sum(counted, axis=1, keepdims=True)
            chunk_exps.append(chunk_exp)
        live = live_down[here]
        weight = live / total
        pos_grad = live * (pos_exp / total - 1.0)
        ps_ref[here, :] = (shared_exp * weight).astype(bf16)
        for other, chunk_exp in zip(starts, chunk_exps):
            pr_ref[here, other : other + part] = (chunk_exp * weight).astype(bf16)
        pull = mul(ps_ref[here, :], shared_rows) + mul(pr_ref[here, :], live_ref[...])
        gl_ref[here, :] = (pos_grad * right_wide + pull).astype(bf16)
        pg_ref[here, :] = pos_grad * left_wide
    left_turned = jnp.transpose(left_ref[...].astype(f32)).astype(bf16)
    place_ref[2] = jnp.transpose(mul(left_turned, ps_ref[...]))
    grad_right = jnp.transpose(mul(left_turned, pr_ref[...])) * live_down + pg_ref[...]
    right_ref[...] = grad_right.astype(bf16)
    slot_down = iota((part, count), 0).astype(f32)
    for kind, source in ((0, gl_ref), (1, right_ref)):
        for start in range(0, slots, part):
            picker = spot_rows[kind][0:1, :] - float(start) == slot_down
            picker = picker.astype(f32).astype(bf16)
            place_ref[kind, start : start + part, :] = mul(picker, source[...])
    for kind in range(3):
        for peer in range(peers):
            leave_ref[peer, pl.ds(bases[kind], cap), :] = place_ref[
                kind, peer * cap : peer * cap + cap, :
            ]
    for peer in range(peers):
        go_ref[peer] = leave_ref[peer, :stride, :].astype(bf16)


def train(info, arrived, count, wide):
    peers, stride, features = arrived.shape
    cap = stride // 3
    slots = peers * cap
    return pl.pallas_call(
        partial(train_kernel, wide),
        out_shape=jax.ShapeDtypeStruct(arrived.shape, bf16),
        in_specs=[in_vmem, in_vmem],
        out_specs=in_vmem,
        scratch_shapes=[
            pltpu.VMEM((peers, stride + cap, features), f32),
            pltpu.VMEM((peers, stride + cap, features), f32),
            pltpu.VMEM((3, slots, features), f32),
            pltpu.VMEM((3, slots, features), f32),
            pltpu.VMEM((count, features), bf16),
            pltpu.VMEM((count, features), bf16),
            pltpu.VMEM((count, features), bf16),
            pltpu.VMEM((count, features), bf16),
            pltpu.VMEM((count, features), f32),
            pltpu.VMEM((count, slots), bf16),
            pltpu.VMEM((count, count), bf16),
        ],
        compiler_params=params(48),
        name="train",
    )(info, arrived)


def update_kernel(
    size, stride, rows_ref, back_ref, table_ref, state_ref, out_hbm, new_state_ref,
    turned, turned_new, grads_ref, out_ref, came, left
):
    peers, wide = rows_ref.shape[1:]
    rows_dev, features = table_ref.shape
    staged = size == stride
    part = min(512, rows_dev)
    parts = rows_dev // part
    per_part = part // lanes

    def come(number):
        rows = pl.ds(pl.multiple_of(number * part, part), part)
        return pltpu.make_async_copy(table_ref.at[rows], out_ref.at[rows], came.at[number])

    if staged:
        for number in range(parts):
            come(number).start()
    asked = block_rows(rows_ref, size, stride) + 64
    length = peers * size
    spread = (iota((wide, length), 0) == iota((wide, length), 1) % size).astype(f32).astype(bf16)
    in_block = iota((peers, length), 1) // size == iota((peers, length), 0)
    flat = [
        jnp.sum(
            jnp.where(in_block, mul(digit.astype(f32).astype(bf16), spread), 0.0),
            axis=0,
            keepdims=True,
        )
        for digit in (asked // 64, asked % 64)
    ]
    flat = (flat[0] * 64.0 + flat[1]).astype(i32) - 64
    state_turned = jnp.transpose(state_ref[...])
    for number in range(parts):
        turned[number, :, :per_part] = state_turned[:, number * per_part : (number + 1) * per_part]

    def leave(number):
        rows = pl.ds(pl.multiple_of(number * part, part), part)
        return pltpu.make_async_copy(out_ref.at[rows], out_hbm.at[rows], left.at[number])

    def finish(number):
        if staged:
            come(number).wait()
        old_ref = out_ref if staged else table_ref
        grads = [grads_ref[j * lanes : (j + 1) * lanes, :] for j in range(per_part)]
        sums = [jnp.sum(g * g, axis=1, keepdims=True) for g in grads]
        state = turned[number, :, :per_part] + jnp.concatenate(sums, axis=1) * (1.0 / features)
        turned_new[number, :, :per_part] = state
        scale = learn_rate / (jnp.sqrt(state) + adagrad_eps)
        for j in range(per_part):
            place = pl.ds(pl.multiple_of(number * part + j * lanes, lanes), lanes)
            out_ref[place, :] = old_ref[place, :] - grads[j] * scale[:, j : j + 1]

    def with_length(length):
        def gather(number):
            picker = flat[:, :length] == iota((part, length), 0) + number * part
            return mul(picker.astype(f32).astype(bf16), back_ref[:length, :])

        def step(number, carry):
            finish(number - 1)
            grads_ref[...] = gather(number)
            leave(number - 1).start()
            return carry

        grads_ref[...] = gather(0)
        lax.fori_loop(1, parts, step, 0)

    if size == stride:
        most = peers * 3 // 4
        few = active_devices(rows_ref) <= most
        pl.when(few)(lambda: with_length(up_to_lanes(most * size)))
        pl.when(jnp.logical_not(few))(lambda: with_length(length))
    else:
        with_length(length)
    finish(parts - 1)
    leave(parts - 1).start()
    for number in range(parts):
        new_state_ref[number * per_part : (number + 1) * per_part, :] = jnp.transpose(
            turned_new[number]
        )[:per_part]
    for number in range(parts):
        leave(number).wait()


def update(rows, returned, table, state, size, stride):
    rows_dev, features = table.shape
    part = min(512, rows_dev)
    parts = rows_dev // part
    new_table, new_state = pl.pallas_call(
        partial(update_kernel, size, stride),
        out_shape=(
            jax.ShapeDtypeStruct(table.shape, f32),
            jax.ShapeDtypeStruct((rows_dev // lanes, lanes), f32),
        ),
        in_specs=[in_vmem, in_vmem, in_hbm if size == stride else in_vmem, in_vmem],
        out_specs=(in_hbm, in_vmem),
        scratch_shapes=[
            pltpu.VMEM((parts, lanes, lanes), f32),
            pltpu.VMEM((parts, lanes, lanes), f32),
            pltpu.VMEM((part, features), f32),
            pltpu.VMEM(table.shape, f32),
            pltpu.SemaphoreType.DMA((parts,)),
            pltpu.SemaphoreType.DMA((parts,)),
        ],
        compiler_params=params(48),
        name="update",
    )(rows, returned, table, state.reshape(rows_dev // lanes, lanes))
    return new_table, new_state.reshape(rows_dev)


def body(
    embeddings,
    adagrad_state,
    edge_count,
    lhs_owner,
    lhs_row,
    rhs_owner,
    rhs_row,
    neg_owner,
    neg_row,
):
    axes = ("dom", "group")
    rows_dev, features = embeddings.shape
    group_len = lhs_row.shape[2]
    group_size = lax.axis_size("group")
    peers = lax.axis_size("dom") * group_size
    stride = 3 * (pl.cdiv(5 * group_len // (4 * peers), 8) * 8)
    half = pl.cdiv(stride // 2, 8) * 8
    sizes = sorted({half, min(half + 16, stride), min(half + 24, stride), stride})
    indices = [
        x.reshape(1, group_len)
        for x in (lhs_owner, lhs_row, rhs_owner, rhs_row, neg_owner, neg_row)
    ]

    def exchange(blocks):
        return lax.all_to_all(blocks, axes, split_axis=0, concat_axis=0, tiled=True)

    def bring(size):
        def run(rows, table16):
            answer = fetch(rows, table16, size, stride).reshape(peers, size, features)
            arrived = exchange(answer)
            if size == stride:
                return arrived
            to_first = [(core, core - 1) for core in range(1, group_size, 2)]
            extra = lax.ppermute(arrived[:, : stride - size], "group", to_first)
            return jnp.concatenate([arrived, extra], axis=1)

        return run

    def take(size):
        def run(rows, grads, table, state):
            over = stride - size
            outgoing = grads
            if over:
                to_second = [(core - 1, core) for core in range(1, group_size, 2)]
                passed = lax.ppermute(grads[:, size:], "group", to_second)
                outgoing = jnp.concatenate(
                    [grads[:, :over] + passed, grads[:, over:size]], axis=1
                )
            returned = exchange(outgoing).reshape(peers * size, features)
            return update(rows, returned, table, state, size, stride)

        return run

    got = exchange(prep(edge_count, indices, peers, stride, rows_dev)).reshape(peers, -1)
    choice, info, rows = plan(got, sizes, stride, rows_dev)
    number = choice[0]
    arrived = lax.switch(
        number, [bring(size) for size in sizes], rows, embeddings.astype(bf16)
    )
    grads = train(info, arrived, group_len, up_to_lanes(stride + 8))
    return lax.switch(
        number, [take(size) for size in sizes], rows, grads, embeddings, adagrad_state
    )


def solution(mesh):
    return jax.shard_map(
        body,
        mesh=mesh,
        in_specs=(
            P(("dom", "group"), None),
            P(("dom", "group")),
            P("dom"),
            P("dom", "group", None, None),
            P("dom", "group", None),
            P("dom", "group", None, None),
            P("dom", "group", None),
            P("dom", "group", None, None),
            P("dom", "group", None),
        ),
        out_specs=(P(("dom", "group"), None), P(("dom", "group"))),
        check_vma=False,
    )
```

```python
from functools import partial

import jax
import jax.numpy as jnp
from jax import lax
from jax.experimental import pallas as pl
from jax.experimental.pallas import tpu as pltpu
from jax.sharding import PartitionSpec as P

learn_rate = 0.1
adagrad_eps = 1e-06
lanes = 128
in_vmem = pl.BlockSpec(memory_space=pltpu.VMEM)
in_smem = pl.BlockSpec(memory_space=pltpu.SMEM)
in_hbm = pl.BlockSpec(memory_space=pltpu.HBM)
by_rows = (((1,), (1,)), ((), ()))
f32, bf16, i32 = jnp.float32, jnp.bfloat16, jnp.int32


def params(mib):
    return pltpu.CompilerParams(vmem_limit_bytes=mib * 2**20)


def mul(a, b):
    return jnp.dot(a, b, preferred_element_type=f32)


def mul_t(a, b):
    return lax.dot_general(a, b, by_rows, preferred_element_type=f32)


def iota(shape, dim):
    return lax.broadcasted_iota(i32, shape, dim)


def prep_kernel(rows_dev, wide, stride, count_hbm, *refs):
    index_hbm, message_ref = refs[:6], refs[6]
    index_refs, edges, arrivals = refs[7:13], refs[13], refs[14]
    copies = [
        pltpu.make_async_copy(source, target, arrivals.at[number])
        for number, (source, target) in enumerate(
            zip((count_hbm, *index_hbm), (edges, *index_refs))
        )
    ]
    for copy in copies:
        copy.start()
    peers = message_ref.shape[0]
    cap = stride // 3
    count = index_refs[0].shape[1]
    part = min(256, count)
    upper = (iota((part, part), 0) < iota((part, part), 1)).astype(f32).astype(bf16)
    peer_of = iota((peers, count), 0)
    slot_of = iota((wide, count), 0).astype(f32)
    for copy in copies:
        copy.wait()
    limit = jnp.clip(edges[0] - lax.axis_index("group") * count, 0, count)
    limit = jnp.full((1, 1), limit, i32)
    live = (iota((1, count), 1) < limit).astype(f32)
    active = (limit > 0).astype(f32)
    match = jnp.concatenate(
        [
            (index_refs[2 * kind][...] == peer_of).astype(f32) * (active if kind == 2 else live)
            for kind in range(3)
        ],
        axis=0,
    )
    seen = jnp.zeros((3 * peers, 1), f32)
    pieces = [[], [], []]
    for start in range(0, count, part):
        now = match[:, start : start + part]
        before = now * (mul(now.astype(bf16), upper) + seen)
        seen = seen + jnp.sum(now, axis=1, keepdims=True)
        for kind in range(3):
            mine = before[kind * peers : kind * peers + peers]
            pieces[kind].append(jnp.sum(mine, axis=0, keepdims=True))
    ranks = [jnp.concatenate(piece, axis=1) for piece in pieces]
    match = match.astype(bf16)
    matches = [match[kind * peers : kind * peers + peers] for kind in range(3)]
    sizes = []
    for kind in range(3):
        most = jnp.max(seen[kind * peers : kind * peers + peers], axis=0, keepdims=True)
        sizes.append(((most.astype(i32) + 7) // 8 * 8).astype(f32))
    starts = [jnp.zeros((1, 1), f32), sizes[0], sizes[0] + sizes[1]]
    found = jnp.zeros((peers, 3 * wide), f32)
    for kind in range(3):
        row = index_refs[2 * kind + 1][...]
        slot = (ranks[kind] + starts[kind] == slot_of).astype(f32)
        digits = [slot * (row // 64).astype(f32), slot * (row % 64).astype(f32), slot]
        found += mul_t(matches[kind], jnp.concatenate(digits, axis=0).astype(bf16))
    high, low, there = [found[:, k * wide : k * wide + wide] for k in range(3)]
    said = jnp.where(there > 0.5, high * 64.0 + low, float(rows_dev))
    lane = iota((peers, wide), 1) - stride
    for number, value in enumerate((starts[2] + sizes[2], limit.astype(f32), starts[1], starts[2])):
        said = jnp.where(lane == number, value, said)
    said = said.astype(i32)
    shared = mul_t(jnp.ones((8, count), bf16), matches[2])[0:1, :]
    shared = shared.astype(i32)
    spots = [
        jnp.where(live > 0.5, index_refs[2 * kind][...].astype(f32) * cap + ranks[kind], 4095.0)
        for kind in range(2)
    ]
    spots = (spots[0] * 4096.0 + spots[1]).astype(i32)
    for peer in range(peers):
        message_ref[peer, :, :wide] = said[peer : peer + 1]
        message_ref[peer, :, wide : wide + peers] = shared
        message_ref[peer, :, message_ref.shape[2] - count :] = spots


def up_to_lanes(size):
    return pl.cdiv(size, lanes) * lanes


def prep(edge_count, indices, peers, stride, rows_dev):
    count = indices[0].shape[1]
    wide = up_to_lanes(stride + 8)
    return pl.pallas_call(
        partial(prep_kernel, rows_dev, wide, stride),
        out_shape=jax.ShapeDtypeStruct((peers, 1, wide + up_to_lanes(peers) + count), i32),
        in_specs=[pl.BlockSpec(memory_space=pl.ANY)] + [in_hbm] * 6,
        out_specs=in_vmem,
        scratch_shapes=[pltpu.VMEM((1, count), i32)] * 6
        + [pltpu.SMEM((1,), i32), pltpu.SemaphoreType.DMA((7,))],
        compiler_params=params(62),
        name="prep",
    )(edge_count, *indices)


def plan_kernel(sizes, wide, stride, rows_dev, got_ref, choice_ref, info_ref, rows_ref):
    peers = got_ref.shape[0]
    chips = peers // 2
    heads = got_ref[:, :wide]
    down = heads[:, stride : stride + 1].astype(f32)
    across = jnp.transpose(jnp.broadcast_to(down, (peers, lanes)))[0:1, :]
    u, t = iota((peers, peers), 0), iota((peers, peers), 1)
    ahead = (down > across) | ((down == across) & (u < t))
    rank = jnp.sum(ahead.astype(f32), axis=0, keepdims=True)
    chip = jnp.where(rank < chips, rank, peers - 1 - rank)
    held = (iota((chips, peers), 0).astype(f32) == chip).astype(f32) * across
    need = jnp.max(jnp.sum(held, axis=1, keepdims=True))
    choice = jnp.int32(0)
    for size in sizes[:-1]:
        choice = choice + (need > 2.0 * size).astype(i32)
    choice_ref[0] = choice
    alone = choice == len(sizes) - 1
    me = lax.axis_index("dom") * lax.axis_size("group") + lax.axis_index("group")
    mine = (me // 2).astype(f32)
    want = jnp.where(me % 2 == 0, mine, peers - 1 - mine)
    want = jnp.where(alone, me.astype(f32), want)
    place = iota((1, peers), 1).astype(f32)
    group = jnp.sum((rank == want).astype(f32) * place).astype(i32)
    first = jnp.sum((rank == mine).astype(f32) * across, axis=1, keepdims=True).astype(i32)
    size = jnp.int32(sizes[0])
    for number in range(1, len(sizes)):
        size = jnp.where(choice == number, sizes[number], size)
    base = (jnp.maximum(first, size) - size) * (me % 2)
    info = got_ref[pl.ds(group, 1), :]
    info = jnp.where(iota(info.shape, 1) == stride + 4, base, info)
    info_ref[...] = jnp.broadcast_to(info, info_ref.shape)
    asked = jnp.where(iota(heads.shape, 1) < stride, heads, rows_dev)
    high, low = (asked // 64).astype(f32).astype(bf16), (asked % 64).astype(f32).astype(bf16)
    chip_down, device_down = (u // 2).astype(f32), u.astype(f32)
    for number, wanted in enumerate((chip_down, peers - 1 - chip_down)):
        chosen = (rank == jnp.where(alone, device_down, wanted)).astype(f32)
        if number == 0:
            sent = jnp.sum(chosen * across, axis=1, keepdims=True)
            sent = jnp.where(alone, jnp.sum((across > 0.0).astype(f32)), sent)
            rows_ref[2] = jnp.broadcast_to(sent, (peers, wide)).astype(i32)
        chosen = chosen.astype(bf16)
        rows_ref[number] = (mul(chosen, high) * 64.0 + mul(chosen, low)).astype(i32)


def plan(got, sizes, stride, rows_dev):
    peers, length = got.shape
    wide = up_to_lanes(stride + 8)
    return pl.pallas_call(
        partial(plan_kernel, sizes, wide, stride, rows_dev),
        out_shape=(
            jax.ShapeDtypeStruct((1,), i32),
            jax.ShapeDtypeStruct((8, length), i32),
            jax.ShapeDtypeStruct((3, peers, wide), i32),
        ),
        in_specs=[in_vmem],
        out_specs=(in_smem, in_vmem, in_vmem),
        compiler_params=params(32),
        name="plan",
    )(got)


def block_rows(rows_ref, size, stride):
    first, second, first_size = rows_ref[0], rows_ref[1], rows_ref[2]
    lane, device = iota(first.shape, 1), iota(first.shape, 0)
    offset = jnp.maximum(first_size, size) - size
    after = second
    for shift in range(8, stride - size + 1, 8):
        after = jnp.where(offset == shift, pltpu.roll(second, shift, 1), after)
    if size < stride:
        rest = pltpu.roll(first, first.shape[1] - size, 1)
        after = jnp.where(lane < offset, rest, after)
    rows = jnp.where(device % 2 == 0, first, after)
    return jnp.where(lane < size, rows, -1)


def fetch_kernel(size, stride, rows_ref, table_ref, out_ref, packed):
    rows_dev = table_ref.shape[0]
    asked = block_rows(rows_ref, size, stride)
    for number in range(packed.shape[0]):
        packed[number] = asked[number * 8 : number * 8 + 8]
    joined = 2 if 16 * size <= 1024 and packed.shape[0] % 2 == 0 else 1
    many = 8 * joined * size
    row_of = iota((many, rows_dev), 1)

    def block(number, carry):
        columns = [jnp.transpose(packed[number * joined + k]) for k in range(joined)]
        column = jnp.concatenate([x[:size, j : j + 1] for x in columns for j in range(8)], axis=0)
        picker = (column == row_of).astype(f32).astype(bf16)
        place = pl.ds(pl.multiple_of(number * many, many), many)
        out_ref[place, :] = mul(picker, table_ref[...]).astype(bf16)
        return carry

    blocks = packed.shape[0] // joined
    if size == stride:
        blocks = pl.cdiv(active_devices(rows_ref), 8)

        def empty(number, carry):
            place = pl.ds(pl.multiple_of(number * 8 * size, 8 * size), 8 * size)
            out_ref[place, :] = jnp.zeros((8 * size, out_ref.shape[1]), bf16)
            return carry

        lax.fori_loop(blocks, packed.shape[0], empty, 0)
    lax.fori_loop(0, blocks, block, 0)


def active_devices(rows_ref):
    return jnp.max(rows_ref[2, 0:1, 0:1].astype(f32)).astype(i32)


def fetch(rows, table, size, stride):
    peers, wide = rows.shape[1:]
    return pl.pallas_call(
        partial(fetch_kernel, size, stride),
        out_shape=jax.ShapeDtypeStruct((peers * size, table.shape[1]), bf16),
        in_specs=[in_vmem, in_vmem],
        out_specs=in_vmem,
        scratch_shapes=[pltpu.VMEM((peers // 8, 8, wide), i32)],
        compiler_params=params(40),
        name="fetch",
    )(rows, table)


def train_kernel(
    wide, info_ref, come_ref, go_ref, stage, leave_ref, wide_ref, place_ref, left_ref, right_ref, live_ref,
    gl_ref, pg_ref, ps_ref, pr_ref
):
    peers, stride, features = come_ref.shape
    cap = stride // 3
    slots = peers * cap
    count = left_ref.shape[0]
    part = min(256, count)
    starts = range(0, count, part)

    def told(number):
        return info_ref[0:1, stride + number : stride + number + 1]

    base = jnp.sum(told(4).astype(f32)).astype(i32)
    bases = [base]
    for number in (2, 3):
        bases.append(base + jnp.sum(told(number).astype(f32)).astype(i32))
    bases = [pl.multiple_of(value, 8) for value in bases]
    for peer in range(peers):
        stage[peer, :stride, :] = come_ref[peer].astype(f32)
        stage[peer, stride:, :] = jnp.zeros((stage.shape[1] - stride, features), f32)

    def lay(kind):
        for peer in range(peers):
            wide_ref[kind, peer * cap : peer * cap + cap, :] = stage[
                peer, pl.ds(bases[kind], cap), :
            ]

    lay(0)
    packed_spots = info_ref[:, info_ref.shape[1] - count :]
    spot_rows = [(packed_spots // 4096).astype(f32), (packed_spots % 4096).astype(f32)]
    spot_columns = [jnp.transpose(rows) for rows in spot_rows]
    shared_down = jnp.transpose(info_ref[:, wide : wide + lanes].astype(f32))[:peers, 0:1]
    place = (iota((peers, slots), 1) - iota((peers, slots), 0) * cap).astype(f32)
    filled = ((place >= 0.0) & (place < shared_down)).astype(f32)
    fill = jnp.sum(filled, axis=0, keepdims=True)
    limit = told(1).astype(f32)
    live_across = (iota((1, count), 1).astype(f32) < limit).astype(f32)
    live_down = (iota((count, 1), 0).astype(f32) < limit).astype(f32)
    slot_across = iota((part, slots), 1).astype(f32)
    for kind, target in ((0, left_ref), (1, right_ref)):
        held = wide_ref[kind].astype(bf16)
        lay(kind + 1)
        half = peers // 2
        cleared = leave_ref.at[kind * half : kind * half + half, :stride, :]
        cleared[...] = jnp.zeros((half, stride, features), f32)
        for start in starts:
            column = spot_columns[kind][start : start + part, 0:1]
            picker = (column == slot_across).astype(f32).astype(bf16)
            rows = mul(picker, held)
            target[start : start + part, :] = rows.astype(bf16)
            if kind == 1:
                rows = rows * live_down[start : start + part]
                live_ref[start : start + part, :] = rows.astype(bf16)
    shared_rows = wide_ref[2].astype(bf16)
    off_diagonal = (iota((part, part), 0) != iota((part, part), 1)).astype(f32)
    for start in starts:
        here = slice(start, start + part)
        left = left_ref[here, :]
        left_wide = left.astype(f32)
        right_wide = right_ref[here, :].astype(f32)
        pos_exp = jnp.exp(jnp.sum(left_wide * right_wide, axis=1, keepdims=True))
        shared_exp = jnp.exp(mul_t(left, shared_rows)) * fill
        total = pos_exp + jnp.sum(shared_exp, axis=1, keepdims=True)
        chunk_exps = []
        for other in starts:
            chunk_exp = jnp.exp(mul_t(left, right_ref[other : other + part, :]))
            if other == start:
                chunk_exp = chunk_exp * off_diagonal
            counted = chunk_exp * live_across[:, other : other + part]
            total = total + jnp.sum(counted, axis=1, keepdims=True)
            chunk_exps.append(chunk_exp)
        live = live_down[here]
        weight = live / total
        pos_grad = live * (pos_exp / total - 1.0)
        ps_ref[here, :] = (shared_exp * weight).astype(bf16)
        for other, chunk_exp in zip(starts, chunk_exps):
            pr_ref[here, other : other + part] = (chunk_exp * weight).astype(bf16)
        pull = mul(ps_ref[here, :], shared_rows) + mul(pr_ref[here, :], live_ref[...])
        gl_ref[here, :] = (pos_grad * right_wide + pull).astype(bf16)
        pg_ref[here, :] = pos_grad * left_wide
    left_turned = jnp.transpose(left_ref[...].astype(f32)).astype(bf16)
    place_ref[2] = jnp.transpose(mul(left_turned, ps_ref[...]))
    grad_right = jnp.transpose(mul(left_turned, pr_ref[...])) * live_down + pg_ref[...]
    right_ref[...] = grad_right.astype(bf16)
    slot_down = iota((part, count), 0).astype(f32)
    for kind, source in ((0, gl_ref), (1, right_ref)):
        for start in range(0, slots, part):
            picker = spot_rows[kind][0:1, :] - float(start) == slot_down
            picker = picker.astype(f32).astype(bf16)
            place_ref[kind, start : start + part, :] = mul(picker, source[...])
    for kind in range(3):
        for peer in range(peers):
            leave_ref[peer, pl.ds(bases[kind], cap), :] = place_ref[
                kind, peer * cap : peer * cap + cap, :
            ]
    for peer in range(peers):
        go_ref[peer] = leave_ref[peer, :stride, :].astype(bf16)


def train(info, arrived, count, wide):
    peers, stride, features = arrived.shape
    cap = stride // 3
    slots = peers * cap
    return pl.pallas_call(
        partial(train_kernel, wide),
        out_shape=jax.ShapeDtypeStruct(arrived.shape, bf16),
        in_specs=[in_vmem, in_vmem],
        out_specs=in_vmem,
        scratch_shapes=[
            pltpu.VMEM((peers, stride + cap, features), f32),
            pltpu.VMEM((peers, stride + cap, features), f32),
            pltpu.VMEM((3, slots, features), f32),
            pltpu.VMEM((3, slots, features), f32),
            pltpu.VMEM((count, features), bf16),
            pltpu.VMEM((count, features), bf16),
            pltpu.VMEM((count, features), bf16),
            pltpu.VMEM((count, features), bf16),
            pltpu.VMEM((count, features), f32),
            pltpu.VMEM((count, slots), bf16),
            pltpu.VMEM((count, count), bf16),
        ],
        compiler_params=params(48),
        name="train",
    )(info, arrived)


def update_kernel(
    size, stride, rows_ref, back_ref, table_ref, state_ref, out_hbm, new_state_ref,
    turned, turned_new, grads_ref, out_ref, came, left
):
    peers, wide = rows_ref.shape[1:]
    rows_dev, features = table_ref.shape
    staged = size == stride
    part = min(512, rows_dev)
    parts = rows_dev // part
    per_part = part // lanes

    def come(number):
        rows = pl.ds(pl.multiple_of(number * part, part), part)
        return pltpu.make_async_copy(table_ref.at[rows], out_ref.at[rows], came.at[number])

    if staged:
        for number in range(parts):
            come(number).start()
    asked = block_rows(rows_ref, size, stride) + 64
    length = peers * size
    spread = (iota((wide, length), 0) == iota((wide, length), 1) % size).astype(f32).astype(bf16)
    in_block = iota((peers, length), 1) // size == iota((peers, length), 0)
    flat = [
        jnp.sum(
            jnp.where(in_block, mul(digit.astype(f32).astype(bf16), spread), 0.0),
            axis=0,
            keepdims=True,
        )
        for digit in (asked // 64, asked % 64)
    ]
    flat = (flat[0] * 64.0 + flat[1]).astype(i32) - 64
    state_turned = jnp.transpose(state_ref[...])
    for number in range(parts):
        turned[number, :, :per_part] = state_turned[:, number * per_part : (number + 1) * per_part]

    def leave(number):
        rows = pl.ds(pl.multiple_of(number * part, part), part)
        return pltpu.make_async_copy(out_ref.at[rows], out_hbm.at[rows], left.at[number])

    def finish(number):
        if staged:
            come(number).wait()
        old_ref = out_ref if staged else table_ref
        grads = [grads_ref[j * lanes : (j + 1) * lanes, :] for j in range(per_part)]
        sums = [jnp.sum(g * g, axis=1, keepdims=True) for g in grads]
        state = turned[number, :, :per_part] + jnp.concatenate(sums, axis=1) * (1.0 / features)
        turned_new[number, :, :per_part] = state
        scale = learn_rate / (jnp.sqrt(state) + adagrad_eps)
        for j in range(per_part):
            place = pl.ds(pl.multiple_of(number * part + j * lanes, lanes), lanes)
            out_ref[place, :] = old_ref[place, :] - grads[j] * scale[:, j : j + 1]

    def with_length(length):
        def gather(number):
            picker = flat[:, :length] == iota((part, length), 0) + number * part
            return mul(picker.astype(f32).astype(bf16), back_ref[:length, :])

        def step(number, carry):
            finish(number - 1)
            grads_ref[...] = gather(number)
            leave(number - 1).start()
            return carry

        grads_ref[...] = gather(0)
        lax.fori_loop(1, parts, step, 0)

    if size == stride:
        most = peers * 3 // 4
        few = active_devices(rows_ref) <= most
        pl.when(few)(lambda: with_length(up_to_lanes(most * size)))
        pl.when(jnp.logical_not(few))(lambda: with_length(length))
    else:
        with_length(length)
    finish(parts - 1)
    leave(parts - 1).start()
    for number in range(parts):
        new_state_ref[number * per_part : (number + 1) * per_part, :] = jnp.transpose(
            turned_new[number]
        )[:per_part]
    for number in range(parts):
        leave(number).wait()


def update(rows, returned, table, state, size, stride):
    rows_dev, features = table.shape
    part = min(512, rows_dev)
    parts = rows_dev // part
    new_table, new_state = pl.pallas_call(
        partial(update_kernel, size, stride),
        out_shape=(
            jax.ShapeDtypeStruct(table.shape, f32),
            jax.ShapeDtypeStruct((rows_dev // lanes, lanes), f32),
        ),
        in_specs=[in_vmem, in_vmem, in_hbm if size == stride else in_vmem, in_vmem],
        out_specs=(in_hbm, in_vmem),
        scratch_shapes=[
            pltpu.VMEM((parts, lanes, lanes), f32),
            pltpu.VMEM((parts, lanes, lanes), f32),
            pltpu.VMEM((part, features), f32),
            pltpu.VMEM(table.shape, f32),
            pltpu.SemaphoreType.DMA((parts,)),
            pltpu.SemaphoreType.DMA((parts,)),
        ],
        compiler_params=params(48),
        name="update",
    )(rows, returned, table, state.reshape(rows_dev // lanes, lanes))
    return new_table, new_state.reshape(rows_dev)


def body(
    embeddings,
    adagrad_state,
    edge_count,
    lhs_owner,
    lhs_row,
    rhs_owner,
    rhs_row,
    neg_owner,
    neg_row,
):
    axes = ("dom", "group")
    rows_dev, features = embeddings.shape
    group_len = lhs_row.shape[2]
    group_size = lax.axis_size("group")
    peers = lax.axis_size("dom") * group_size
    stride = 3 * (pl.cdiv(5 * group_len // (4 * peers), 8) * 8)
    half = pl.cdiv(stride // 2, 8) * 8
    sizes = sorted({half, min(half + 16, stride), min(half + 24, stride), stride})
    indices = [
        x.reshape(1, group_len)
        for x in (lhs_owner, lhs_row, rhs_owner, rhs_row, neg_owner, neg_row)
    ]

    def exchange(blocks):
        return lax.all_to_all(blocks, axes, split_axis=0, concat_axis=0, tiled=True)

    def bring(size):
        def run(rows, table16):
            answer = fetch(rows, table16, size, stride).reshape(peers, size, features)
            arrived = exchange(answer)
            if size == stride:
                return arrived
            to_first = [(core, core - 1) for core in range(1, group_size, 2)]
            extra = lax.ppermute(arrived[:, : stride - size], "group", to_first)
            return jnp.concatenate([arrived, extra], axis=1)

        return run

    def take(size):
        def run(rows, grads, table, state):
            over = stride - size
            outgoing = grads
            if over:
                to_second = [(core - 1, core) for core in range(1, group_size, 2)]
                passed = lax.ppermute(grads[:, size:], "group", to_second)
                outgoing = jnp.concatenate(
                    [grads[:, :over] + passed, grads[:, over:size]], axis=1
                )
            returned = exchange(outgoing).reshape(peers * size, features)
            return update(rows, returned, table, state, size, stride)

        return run

    got = exchange(prep(edge_count, indices, peers, stride, rows_dev)).reshape(peers, -1)
    choice, info, rows = plan(got, sizes, stride, rows_dev)
    number = choice[0]
    arrived = lax.switch(
        number, [bring(size) for size in sizes], rows, embeddings.astype(bf16)
    )
    grads = train(info, arrived, group_len, up_to_lanes(stride + 8))
    return lax.switch(
        number, [take(size) for size in sizes], rows, grads, embeddings, adagrad_state
    )


def solution(mesh):
    return jax.shard_map(
        body,
        mesh=mesh,
        in_specs=(
            P(("dom", "group"), None),
            P(("dom", "group")),
            P("dom"),
            P("dom", "group", None, None),
            P("dom", "group", None),
            P("dom", "group", None, None),
            P("dom", "group", None),
            P("dom", "group", None, None),
            P("dom", "group", None),
        ),
        out_specs=(P(("dom", "group"), None), P(("dom", "group"))),
        check_vma=False,
    )
```
